128 devices in a mesh: ctx: 32 (over x, y_lo, z), sub: 4 (over y_hi, core).
Axes of the slice: x: 4, y: 4 (y_hi: 2, y_lo: 2; y = y_hi * 2 + y_lo), z: 4, core: 2. Of those that a mesh axis runs over, the one named last changes fastest.
Arguments:
- queries: bfloat16 [128, 65536], P(None, ('ctx', 'sub')), may hold values from -6 to 6
- key_branch: bfloat16 [128, 65536], P(None, ('ctx', 'sub')), may hold values from -6 to 6
- value_branch: bfloat16 [128, 65536], P(None, ('ctx', 'sub')), may hold values from -6 to 6
- out_grad: bfloat16 [128, 65536], P(None, ('ctx', 'sub')), as said below
- residue: float32 [128, 16], P(('ctx', 'sub')), as said below
- log_rate: float32 [128, 16], P(('ctx', 'sub')), as said below
- skip_gain: float32 [128], replicated, may hold values from 0.5 to 1.5
Outputs:
- output: bfloat16 [128, 65536], P(None, ('ctx', 'sub'))
- grad_query: bfloat16 [128, 65536], P(None, ('ctx', 'sub'))
- grad_key: bfloat16 [128, 65536], P(None, ('ctx', 'sub'))
- grad_value: bfloat16 [128, 65536], P(None, ('ctx', 'sub'))
- grad_residue: float32 [128, 16], P(('ctx', 'sub'))
- grad_log_rate: float32 [128, 16], P(('ctx', 'sub'))
- grad_skip: float32 [128], P(('ctx', 'sub'))
The draws below stay inside these ranges and needn't reach their ends.
Inputs may be any that keep to these rules, and one draw needn't show every extreme that they name: `out_grad`: each entry lies between -18 and 18. exp(log_rate) lies between 0.2 / 65536 and 0.1. `residue`: real-valued residues.
All inputs are finite; a program needn't handle non-finite values.
Results may differ from the reference program's by a relative error of at most 0.027.
Values may be sent and summed in bfloat16 or wider, within the bound.
A program may use at most 128 MiB of HBM per device.

```python
import math
import jax
import jax.numpy as jnp
from jax import lax

CH = 128
MODES = 16
NSEQ = 65536


def mode_rates(base_key, slow_share):
    pick_key, slow_key, fast_key = jax.random.split(base_key, 3)
    is_slow = jax.random.uniform(pick_key, (CH, MODES)) < slow_share
    slow_rate = jax.random.uniform(slow_key, (CH, MODES), minval=0.2, maxval=2.0) / NSEQ
    fast_rate = jnp.exp(jax.random.uniform(fast_key, (CH, MODES), minval=math.log(0.02), maxval=math.log(0.1)))
    return jnp.where(is_slow, slow_rate, fast_rate)


def draw_log_rate(key, part):
    slow_share = 0.5
    return jnp.log(mode_rates(key, slow_share)).astype(jnp.float32)


def draw_residue(key, part):
    slow_share = 0.5
    decay_rate = mode_rates(key, slow_share)
    key = jax.random.fold_in(key, 11)
    base_draw = jax.random.normal(key, (CH, MODES))
    return (base_draw * jnp.sqrt(2.0 * jnp.maximum(decay_rate, 1.0 / NSEQ) / MODES)).astype(jnp.float32)


def draw_out_grad(key, part):
    key = jax.random.fold_in(key, 23)
    time_ramp = 1.0 + 2.0 * jnp.arange(NSEQ, dtype=jnp.int32).astype(jnp.float32) / NSEQ
    base_draw = jnp.clip(jax.random.normal(key, (CH, NSEQ)), -6.0, 6.0)
    return (base_draw * time_ramp[None, :]).astype(jnp.bfloat16)


def levels(key, extent, shards, smallest, high):
    gain, own = 1.0, jax.random.fold_in(key, 6)
    for dim, shards_of in shards:
        draws = jnp.exp(jax.random.uniform(jax.random.fold_in(own, dim), (shards_of,), jnp.float32, smallest / len(shards), high / len(shards)))
        gain = gain * jnp.repeat(draws, extent[dim] // shards_of).reshape([-1 if axis == dim else 1 for axis in range(len(extent))])
    return gain


def centred(rng, dims, width, most, shards=(), kind=jnp.bfloat16):
    values = width * jax.random.normal(rng, dims, jnp.float32)
    if shards:
        values = values * levels(rng, dims, shards, -0.22, 0.18)
    return jnp.clip(values, -most, most).astype(kind)


def setup_inputs(seed: int = 0) -> dict:
    streams_of = jax.random.split(jax.random.key(seed), 8)
    queries = centred(streams_of[0], (CH, NSEQ), 1.0, 6.0, ((1, 128),))
    key_branch = centred(streams_of[1], (CH, NSEQ), 1.0, 6.0, ((1, 128),))
    value_branch = centred(streams_of[2], (CH, NSEQ), 1.0, 6.0, ((1, 128),))
    out_grad = draw_out_grad(jax.random.fold_in(streams_of[7], 71), 0)
    residue = draw_residue(jax.random.fold_in(streams_of[7], 71), 0)
    log_rate = draw_log_rate(jax.random.fold_in(streams_of[7], 71), 0)
    skip_gain = jnp.clip(jax.random.uniform(streams_of[6], (CH,), jnp.float32, 0.5, 1.5), 0.5, 1.5)
    return {"queries": queries, "key_branch": key_branch, "value_branch": value_branch, "out_grad": out_grad, "residue": residue, "log_rate": log_rate, "skip_gain": skip_gain}


def reference(queries, key_branch, value_branch, out_grad, residue, log_rate, skip_gain):
    mixed = (key_branch.astype(jnp.float32) * value_branch.astype(jnp.float32)).astype(jnp.bfloat16)
    gated = (out_grad.astype(jnp.float32) * queries.astype(jnp.float32)).astype(jnp.bfloat16)
    padded_len = 2 * NSEQ
    positions = jnp.arange(NSEQ, dtype=jnp.int32).astype(jnp.float32)
    decay_rate = jnp.exp(log_rate)
    group_size = 4

    def per_group(inputs):
        mix_rows, gate_rows, res_rows, rate_rows = inputs
        decay = jnp.exp(-rate_rows[:, :, None] * positions[None, None, :])
        filt = lax.optimization_barrier(jnp.sum(res_rows[:, :, None] * decay, axis=1))
        spec_filt = jnp.fft.rfft(filt, n=padded_len, axis=-1)
        spec_in = jnp.fft.rfft(mix_rows.astype(jnp.float32), n=padded_len, axis=-1)
        spec_grad = jnp.fft.rfft(gate_rows.astype(jnp.float32), n=padded_len, axis=-1)
        conv_part = jnp.fft.irfft(spec_in * spec_filt, n=padded_len, axis=-1)[:, :NSEQ]
        corr_part = jnp.fft.irfft(jnp.conj(spec_filt) * spec_grad, n=padded_len, axis=-1)[:, :NSEQ]
        lag_grad = jnp.fft.irfft(jnp.conj(spec_in) * spec_grad, n=padded_len, axis=-1)[:, :NSEQ]
        plain_sums = lax.optimization_barrier(jnp.sum(lag_grad[:, None, :] * decay, axis=2))
        timed_sums = lax.optimization_barrier(jnp.sum(lag_grad[:, None, :] * decay * positions[None, None, :], axis=2))
        return (conv_part, corr_part, plain_sums / NSEQ, -res_rows * rate_rows * timed_sums / math.sqrt(NSEQ))
    groups = CH // group_size
    shaped = (mixed.reshape(groups, group_size, NSEQ), gated.reshape(groups, group_size, NSEQ), residue.reshape(groups, group_size, MODES), decay_rate.reshape(groups, group_size, MODES))
    conv_part, corr_part, grad_residue, grad_log_rate = lax.map(per_group, shaped)
    conv_part = conv_part.reshape(CH, NSEQ)
    corr_part = corr_part.reshape(CH, NSEQ)
    gain_col = skip_gain[:, None]
    forward_sum = conv_part + gain_col * mixed.astype(jnp.float32)
    input_grad = corr_part + gain_col * gated.astype(jnp.float32)
    output = (queries.astype(jnp.float32) * forward_sum).astype(jnp.bfloat16)
    grad_query = (out_grad.astype(jnp.float32) * forward_sum).astype(jnp.bfloat16)
    grad_key = (input_grad * value_branch.astype(jnp.float32)).astype(jnp.bfloat16)
    grad_value = (input_grad * key_branch.astype(jnp.float32)).astype(jnp.bfloat16)
    grad_skip = lax.optimization_barrier(jnp.sum(gated.astype(jnp.float32) * mixed.astype(jnp.float32), axis=1))
    return (output, grad_query, grad_key, grad_value, grad_residue.reshape(CH, MODES), grad_log_rate.reshape(CH, MODES), grad_skip)
```

```python
import functools

import jax
import jax.numpy as jnp
from jax import lax
from jax.experimental import pallas as pl
from jax.experimental.pallas import tpu as pltpu
from jax.sharding import PartitionSpec as P

MESH = pl.DeviceIdType.MESH
FULL = lax.Precision.HIGHEST
NT = (((1,), (1,)), ((), ()))
TN = (((0,), (0,)), ((), ()))
LANES = 128


def iota(shape, axis):
    return lax.broadcasted_iota(jnp.int32, shape, axis)


def column(row):
    n = row.shape[1]
    eye = iota((n, n), 0) == iota((n, n), 1)
    return jnp.sum(jnp.where(eye, row, 0.0), axis=1, keepdims=True)


def shifted(rows, count):
    n = rows.shape[0]
    if count > 0:
        moved = pltpu.roll(rows, count, 0)
        return jnp.where(iota(rows.shape, 0) >= count, moved, 0.0)
    moved = pltpu.roll(rows, n + count, 0)
    return jnp.where(iota(rows.shape, 0) < n + count, moved, 0.0)


def running(rows, speed, span, sign):
    n = rows.shape[0]
    step = 1
    while step < n:
        rows = rows + jnp.exp(-speed * float(span * step)) * shifted(rows, sign * step)
        step *= 2
    return shifted(rows, sign)


def send_all(devices, sub, me, src, dst, send_sem, recv_sem):
    def one(k, carry):
        peer = lax.rem(me + k, devices)
        pltpu.make_async_remote_copy(
            src_ref=src.at[peer],
            dst_ref=dst.at[me],
            send_sem=send_sem,
            recv_sem=recv_sem,
            device_id=(peer // sub, lax.rem(peer, sub)),
            device_id_type=MESH,
        ).start()
        return carry

    lax.fori_loop(1, devices, one, 0)


def whole(devices, sub, me, src, dst, send_sem, recv_sem):
    peer = lax.rem(me + 1, devices)
    return pltpu.make_async_remote_copy(
        src_ref=src.at[pl.ds(0, devices - 1)],
        dst_ref=dst.at[pl.ds(0, devices - 1)],
        send_sem=send_sem,
        recv_sem=recv_sem,
        device_id=(peer // sub, lax.rem(peer, sub)),
        device_id_type=MESH,
    )


def exchange_kernel(
    devices, sub, q_ref, k_ref, v_ref, og_ref, res_ref, rate_ref,
    conv_ref, corr_ref, row_ref,
    stage, toep, out_buf, in_buf, back_buf, home_buf,
    out_send, out_recv, back_send, back_recv,
):
    me = lax.axis_index("ctx") * sub + lax.axis_index("sub")
    channels, width = q_ref.shape
    blocks = width // LANES
    slab = 2 * blocks
    modes = res_ref.shape[1]
    barrier = pltpu.get_barrier_semaphore()

    def greet(k, carry):
        peer = lax.rem(me + k, devices)
        pl.semaphore_signal(
            barrier, inc=1, device_id=(peer // sub, lax.rem(peer, sub)), device_id_type=MESH
        )
        return carry

    lax.fori_loop(1, devices, greet, 0)

    f32, bf16 = jnp.float32, jnp.bfloat16

    def spread(first, second):
        for j in range(blocks):
            cols = slice(j * LANES, (j + 1) * LANES)
            stage[pl.ds(j, channels, stride=slab), :] = first(cols)
            stage[pl.ds(blocks + j, channels, stride=slab), :] = second(cols)
        return stage[...].astype(bf16).reshape(channels, slab, LANES)

    out_buf[...] = spread(
        lambda c: k_ref[:, c].astype(f32) * v_ref[:, c].astype(f32),
        lambda c: og_ref[:, c].astype(f32) * q_ref[:, c].astype(f32),
    )
    pl.semaphore_wait(barrier, devices - 1)
    send_all(devices, sub, me, out_buf, in_buf, out_send, out_recv)
    in_buf[me] = out_buf[me]

    speed_row = jnp.exp(rate_ref[...])
    res_row = res_ref[...]
    speed = column(speed_row)
    res = column(res_row)
    pos = iota((modes, width), 1).astype(f32)
    rise = jnp.exp(-speed * pos)
    fall = jnp.exp(-speed * (width - 1.0 - pos))
    to_end = fall.astype(bf16)
    to_end_timed = (fall * (width - 1.0 - pos)).astype(bf16)
    to_start = rise.astype(bf16)
    to_start_timed = (rise * pos).astype(bf16)
    from_before = (res * jnp.exp(-speed * (pos + 1.0))).astype(bf16)
    from_after = (res * jnp.exp(-speed * (width - pos))).astype(bf16)
    grow = jnp.exp(speed * iota((modes, LANES), 1).astype(f32))
    lag = iota((LANES, width), 1) - iota((LANES, width), 0)
    near = lax.dot_general(grow, res * rise, TN, precision=FULL, preferred_element_type=f32)
    near = jnp.where(lag >= 0, near, 0.0).astype(bf16)
    for row in range(blocks):
        rows = slice(row * LANES, (row + 1) * LANES)
        if row:
            toep[rows, : row * LANES] = jnp.zeros((LANES, row * LANES), bf16)
        toep[rows, row * LANES :] = near[:, : width - row * LANES]

    whole(devices, sub, me, out_buf, in_buf, out_send, out_recv).wait_recv()
    stage[...] = in_buf[...].reshape(devices * slab, LANES).astype(f32)

    def gathered(start):
        parts = [stage[pl.ds(start + j, devices, stride=slab), :] for j in range(blocks)]
        return jnp.concatenate(parts, axis=1).astype(bf16)

    mixed, gated = gathered(0), gathered(blocks)

    def state(rows, weights):
        return lax.dot_general(rows, weights, NT, preferred_element_type=f32)

    ends, starts = state(mixed, to_end), state(gated, to_start)
    before = running(ends, speed_row, width, 1)
    after = running(starts, speed_row, width, -1)
    conv = jnp.dot(mixed, toep[...], preferred_element_type=f32)
    conv = conv + jnp.dot(before.astype(bf16), from_before, preferred_element_type=f32)
    corr = lax.dot_general(gated, toep[...], NT, preferred_element_type=f32)
    corr = corr + jnp.dot(after.astype(bf16), from_after, preferred_element_type=f32)
    back_buf[...] = spread(lambda c: conv[:, c], lambda c: corr[:, c])
    send_all(devices, sub, me, back_buf, home_buf, back_send, back_recv)
    home_buf[me] = back_buf[me]

    pairs = lax.dot_general(mixed, gated, TN, preferred_element_type=f32)
    lagged = []
    for k in range(blocks):
        total = pairs[:LANES, k * LANES : (k + 1) * LANES]
        for row in range(1, blocks - k):
            rows = slice(row * LANES, (row + 1) * LANES)
            total = total + pairs[rows, (row + k) * LANES : (row + k + 1) * LANES]
        lagged.append(total)
    lagged = jnp.where(lag >= 0, jnp.concatenate(lagged, axis=1), 0.0)
    skip_sum = jnp.sum(jnp.where(lag == 0, lagged, 0.0), keepdims=True)

    def local_sum(values):
        by_lag = jnp.dot(grow, values, precision=FULL, preferred_element_type=f32)
        return jnp.sum(by_lag * rise, axis=1, keepdims=True)

    plain_col = local_sum(lagged)
    timed_col = local_sum(lagged * lag.astype(f32))
    eye = iota((modes, modes), 0) == iota((modes, modes), 1)

    def as_row(col):
        return jnp.sum(jnp.where(eye, col, 0.0), axis=0, keepdims=True)

    one_step = jnp.exp(-speed_row)
    chunk_step = jnp.exp(-speed_row * float(width))
    ends_timed, starts_timed = state(mixed, to_end_timed), state(gated, to_start_timed)
    cross = before * starts
    cross_timed = ends_timed * after + before * starts_timed + cross
    cross_timed = cross_timed + (float(width) * chunk_step) * (before * after)
    plain = as_row(plain_col) + one_step * jnp.sum(cross, axis=0, keepdims=True)
    timed = as_row(timed_col) + one_step * jnp.sum(cross_timed, axis=0, keepdims=True)
    seq_len = devices * width
    row_ref[0:1, :] = jnp.zeros((1, LANES), f32)
    row_ref[0:1, 0:modes] = plain * (1.0 / seq_len)
    row_ref[0:1, modes : 2 * modes] = -res_row * speed_row * timed * (1.0 / seq_len**0.5)
    row_ref[0:1, 2 * modes : 2 * modes + 1] = skip_sum

    whole(devices, sub, me, back_buf, home_buf, back_send, back_recv).wait_recv()
    stage[...] = home_buf[...].reshape(channels * slab, LANES).astype(f32)
    for j in range(blocks):
        cols = slice(j * LANES, (j + 1) * LANES)
        conv_ref[:, cols] = stage[pl.ds(j, channels, stride=slab), :].astype(bf16)
        corr_ref[:, cols] = stage[pl.ds(blocks + j, channels, stride=slab), :].astype(bf16)
    whole(devices, sub, me, out_buf, in_buf, out_send, out_recv).wait_send()
    whole(devices, sub, me, back_buf, home_buf, back_send, back_recv).wait_send()


def finish_kernel(
    q_ref, k_ref, v_ref, og_ref, gain_ref, conv_ref, corr_ref, row_ref,
    out_ref, gq_ref, gk_ref, gv_ref, gres_ref, grate_ref, gskip_ref,
):
    f32, bf16 = jnp.float32, jnp.bfloat16
    modes = gres_ref.shape[1]
    gain = column(gain_ref[...])
    q, k = q_ref[...].astype(f32), k_ref[...].astype(f32)
    v, og = v_ref[...].astype(f32), og_ref[...].astype(f32)
    mixed = (k * v).astype(bf16).astype(f32)
    gated = (og * q).astype(bf16).astype(f32)
    forward_sum = conv_ref[...].astype(f32) + gain * mixed
    input_grad = corr_ref[...].astype(f32) + gain * gated
    out_ref[...] = (q * forward_sum).astype(bf16)
    gq_ref[...] = (og * forward_sum).astype(bf16)
    gk_ref[...] = (input_grad * v).astype(bf16)
    gv_ref[...] = (input_grad * k).astype(bf16)
    gres_ref[...] = row_ref[:, 0:modes]
    grate_ref[...] = row_ref[:, modes : 2 * modes]
    gskip_ref[...] = row_ref[:, 2 * modes : 2 * modes + 1]


def body(queries, key_branch, value_branch, out_grad, residue, log_rate, skip_gain):
    sub = lax.axis_size("sub")
    devices = lax.axis_size("ctx") * sub
    channels, width = queries.shape
    modes = residue.shape[1]
    slab = 2 * width // LANES
    f32, bf16 = jnp.float32, jnp.bfloat16
    vmem = pl.BlockSpec(memory_space=pltpu.VMEM)
    wide = jax.ShapeDtypeStruct((channels, width), bf16)
    conv, corr, row = pl.pallas_call(
        functools.partial(exchange_kernel, devices, sub),
        out_shape=(wide, wide, jax.ShapeDtypeStruct((1, LANES), f32)),
        in_specs=[vmem] * 6,
        out_specs=(vmem,) * 3,
        scratch_shapes=[
            pltpu.VMEM((channels * slab, LANES), f32),
            pltpu.VMEM((width, width), bf16),
            pltpu.VMEM((channels, slab, LANES), bf16),
            pltpu.VMEM((devices, slab, LANES), bf16),
            pltpu.VMEM((devices, slab, LANES), bf16),
            pltpu.VMEM((channels, slab, LANES), bf16),
            pltpu.SemaphoreType.DMA,
            pltpu.SemaphoreType.DMA,
            pltpu.SemaphoreType.DMA,
            pltpu.SemaphoreType.DMA,
        ],
        compiler_params=pltpu.CompilerParams(
            collective_id=0, has_side_effects=True, vmem_limit_bytes=32 * 2**20
        ),
        name="exchange",
    )(queries, key_branch, value_branch, out_grad, residue, log_rate)
    output, grad_query, grad_key, grad_value, grad_residue, grad_rate, grad_skip = pl.pallas_call(
        finish_kernel,
        out_shape=(wide,) * 4
        + (jax.ShapeDtypeStruct((1, modes), f32),) * 2
        + (jax.ShapeDtypeStruct((1, 1), f32),),
        in_specs=[vmem] * 8,
        out_specs=(vmem,) * 7,
        compiler_params=pltpu.CompilerParams(vmem_limit_bytes=32 * 2**20),
        name="finish",
    )(queries, key_branch, value_branch, out_grad, skip_gain[None, :], conv, corr, row)
    return (
        output, grad_query, grad_key, grad_value, grad_residue, grad_rate, grad_skip.reshape(1)
    )


def solution(mesh):
    wide = P(None, ("ctx", "sub"))
    rows = P(("ctx", "sub"), None)
    return jax.shard_map(
        body,
        mesh=mesh,
        in_specs=(wide, wide, wide, wide, rows, rows, P()),
        out_specs=(wide, wide, wide, wide, rows, rows, P(("ctx", "sub"))),
        check_vma=False,
    )
```

```python
import functools

import jax
import jax.numpy as jnp
from jax import lax
from jax.experimental import pallas as pl
from jax.experimental.pallas import tpu as pltpu
from jax.sharding import PartitionSpec as P

MESH = pl.DeviceIdType.MESH
FULL = lax.Precision.HIGHEST
NT = (((1,), (1,)), ((), ()))
TN = (((0,), (0,)), ((), ()))
LANES = 128


def iota(shape, axis):
    return lax.broadcasted_iota(jnp.int32, shape, axis)


def column(row):
    n = row.shape[1]
    eye = iota((n, n), 0) == iota((n, n), 1)
    return jnp.sum(jnp.where(eye, row, 0.0), axis=1, keepdims=True)


def shifted(rows, count):
    n = rows.shape[0]
    if count > 0:
        moved = pltpu.roll(rows, count, 0)
        return jnp.where(iota(rows.shape, 0) >= count, moved, 0.0)
    moved = pltpu.roll(rows, n + count, 0)
    return jnp.where(iota(rows.shape, 0) < n + count, moved, 0.0)


def running(rows, speed, span, sign):
    n = rows.shape[0]
    step = 1
    while step < n:
        rows = rows + jnp.exp(-speed * float(span * step)) * shifted(rows, sign * step)
        step *= 2
    return shifted(rows, sign)


def partners(me):
    core, z = me % 2, me // 4 % 4
    y, x = me // 2 % 2 * 2 + me // 16 % 2, me // 32
    across = [lax.rem(x + d, 4) * 8 for d in range(4)]
    along = [lax.rem(z + d, 4) for d in range(4)]
    ups = [lax.rem(y + d, 4) for d in range(4)]
    high = [[u // 2 * 2 + lax.rem(core + d, 2) for d in range(2)] for u in ups]
    low = [lax.rem(u, 2) * 4 for u in ups]
    moves = [
        (dx, dy, dz, dc)
        for dx in range(4) for dy in range(4) for dz in range(4) for dc in range(2)
        if (dx, dy, dz, dc) != (0, 0, 0, 0)
    ]
    moves.sort(key=lambda m: -sum(min(d, 4 - d) for d in m[:3]))
    found = []
    for dx, dy, dz, dc in moves:
        ctx, sub = across[dx] + low[dy] + along[dz], high[dy][dc]
        found.append((ctx * 4 + sub, (ctx, sub)))
    return found


def send_all(peers, me, src, dst, send_sem, recv_sem):
    for peer, place in peers:
        pltpu.make_async_remote_copy(
            src_ref=src.at[peer],
            dst_ref=dst.at[me],
            send_sem=send_sem,
            recv_sem=recv_sem,
            device_id=place,
            device_id_type=MESH,
        ).start()


def whole(peers, src, dst, send_sem, recv_sem):
    return pltpu.make_async_remote_copy(
        src_ref=src.at[pl.ds(0, len(peers))],
        dst_ref=dst.at[pl.ds(0, len(peers))],
        send_sem=send_sem,
        recv_sem=recv_sem,
        device_id=peers[0][1],
        device_id_type=MESH,
    )


def exchange_kernel(
    devices, sub, q_hbm, k_hbm, v_hbm, og_hbm, res_hbm, rate_hbm, gain_hbm,
    conv_ref, corr_ref, row_ref, q_ref, k_ref, v_ref, og_ref, gain_ref,
    res_ref, rate_ref, stage, toep, out_buf, in_buf, back_buf, home_buf,
    load_sems, out_send, out_recv, back_send, back_recv,
):
    me = lax.axis_index("ctx") * sub + lax.axis_index("sub")
    channels, width = q_ref.shape
    blocks = width // LANES
    slab = 2 * blocks
    modes = res_ref.shape[1]
    peers = partners(me)
    barrier = pltpu.get_barrier_semaphore()
    for _, place in peers:
        pl.semaphore_signal(barrier, inc=1, device_id=place, device_id_type=MESH)
    loads = [
        pltpu.make_async_copy(src, dst, load_sems.at[i])
        for i, (src, dst) in enumerate(
            [(k_hbm, k_ref), (v_hbm, v_ref), (og_hbm, og_ref), (q_hbm, q_ref),
             (res_hbm, res_ref), (rate_hbm, rate_ref), (gain_hbm, gain_ref)]
        )
    ]
    for load in loads:
        load.start()
    for load in loads:
        load.wait()

    f32, bf16 = jnp.float32, jnp.bfloat16

    def spread(first, second):
        for j in range(blocks):
            cols = slice(j * LANES, (j + 1) * LANES)
            stage[pl.ds(j, channels, stride=slab), :] = first(cols)
            stage[pl.ds(blocks + j, channels, stride=slab), :] = second(cols)
        return stage[...].astype(bf16).reshape(channels, slab, LANES)

    out_buf[...] = spread(
        lambda c: k_ref[:, c].astype(f32) * v_ref[:, c].astype(f32),
        lambda c: og_ref[:, c].astype(f32) * q_ref[:, c].astype(f32),
    )
    pl.semaphore_wait(barrier, devices - 1)
    send_all(peers, me, out_buf, in_buf, out_send, out_recv)
    in_buf[me] = out_buf[me]

    speed_row = jnp.exp(rate_ref[...])
    res_row = res_ref[...]
    speed = column(speed_row)
    res = column(res_row)
    pos = iota((modes, width), 1).astype(f32)
    rise = jnp.exp(-speed * pos)
    fall = jnp.exp(-speed * (width - 1.0 - pos))
    to_end = fall.astype(bf16)
    to_end_timed = (fall * (width - 1.0 - pos)).astype(bf16)
    to_start = rise.astype(bf16)
    to_start_timed = (rise * pos).astype(bf16)
    from_before = (res * jnp.exp(-speed * (pos + 1.0))).astype(bf16)
    from_after = (res * jnp.exp(-speed * (width - pos))).astype(bf16)
    grow = jnp.exp(speed * iota((modes, LANES), 1).astype(f32))
    lag = iota((LANES, width), 1) - iota((LANES, width), 0)
    near = lax.dot_general(grow, res * rise, TN, precision=FULL, preferred_element_type=f32)
    near = jnp.where(lag >= 0, near, 0.0).astype(bf16)
    for row in range(blocks):
        rows = slice(row * LANES, (row + 1) * LANES)
        if row:
            toep[rows, : row * LANES] = jnp.zeros((LANES, row * LANES), bf16)
        toep[rows, row * LANES :] = near[:, : width - row * LANES]

    whole(peers, out_buf, in_buf, out_send, out_recv).wait_recv()
    stage[...] = in_buf[...].reshape(devices * slab, LANES).astype(f32)

    def gathered(start):
        parts = [stage[pl.ds(start + j, devices, stride=slab), :] for j in range(blocks)]
        return jnp.concatenate(parts, axis=1).astype(bf16)

    mixed, gated = gathered(0), gathered(blocks)

    def state(rows, weights):
        return lax.dot_general(rows, weights, NT, preferred_element_type=f32)

    ends, starts = state(mixed, to_end), state(gated, to_start)
    before = running(ends, speed_row, width, 1)
    after = running(starts, speed_row, width, -1)
    conv = jnp.dot(mixed, toep[...], preferred_element_type=f32)
    conv = conv + jnp.dot(before.astype(bf16), from_before, preferred_element_type=f32)
    corr = lax.dot_general(gated, toep[...], NT, preferred_element_type=f32)
    corr = corr + jnp.dot(after.astype(bf16), from_after, preferred_element_type=f32)
    back_buf[...] = spread(lambda c: conv[:, c], lambda c: corr[:, c])
    send_all(peers, me, back_buf, home_buf, back_send, back_recv)
    home_buf[me] = back_buf[me]

    pairs = lax.dot_general(mixed, gated, TN, preferred_element_type=f32)
    lagged = []
    for k in range(blocks):
        total = pairs[:LANES, k * LANES : (k + 1) * LANES]
        for row in range(1, blocks - k):
            rows = slice(row * LANES, (row + 1) * LANES)
            total = total + pairs[rows, (row + k) * LANES : (row + k + 1) * LANES]
        lagged.append(total)
    lagged = jnp.where(lag >= 0, jnp.concatenate(lagged, axis=1), 0.0)
    skip_sum = jnp.sum(jnp.where(lag == 0, lagged, 0.0), keepdims=True)

    def local_sum(values):
        by_lag = jnp.dot(grow, values, precision=FULL, preferred_element_type=f32)
        return jnp.sum(by_lag * rise, axis=1, keepdims=True)

    plain_col = local_sum(lagged)
    timed_col = local_sum(lagged * lag.astype(f32))
    eye = iota((modes, modes), 0) == iota((modes, modes), 1)

    def as_row(col):
        return jnp.sum(jnp.where(eye, col, 0.0), axis=0, keepdims=True)

    one_step = jnp.exp(-speed_row)
    chunk_step = jnp.exp(-speed_row * float(width))
    ends_timed, starts_timed = state(mixed, to_end_timed), state(gated, to_start_timed)
    cross = before * starts
    cross_timed = ends_timed * after + before * starts_timed + cross
    cross_timed = cross_timed + (float(width) * chunk_step) * (before * after)
    plain = as_row(plain_col) + one_step * jnp.sum(cross, axis=0, keepdims=True)
    timed = as_row(timed_col) + one_step * jnp.sum(cross_timed, axis=0, keepdims=True)
    seq_len = devices * width
    row_ref[0:1, :] = jnp.zeros((1, LANES), f32)
    row_ref[0:1, 0:modes] = plain * (1.0 / seq_len)
    row_ref[0:1, modes : 2 * modes] = -res_row * speed_row * timed * (1.0 / seq_len**0.5)
    row_ref[0:1, 2 * modes : 2 * modes + 1] = skip_sum

    whole(peers, back_buf, home_buf, back_send, back_recv).wait_recv()
    stage[...] = home_buf[...].reshape(channels * slab, LANES).astype(f32)
    for j in range(blocks):
        cols = slice(j * LANES, (j + 1) * LANES)
        conv_ref[:, cols] = stage[pl.ds(j, channels, stride=slab), :].astype(bf16)
        corr_ref[:, cols] = stage[pl.ds(blocks + j, channels, stride=slab), :].astype(bf16)
    whole(peers, out_buf, in_buf, out_send, out_recv).wait_send()
    whole(peers, back_buf, home_buf, back_send, back_recv).wait_send()


def finish_kernel(
    q_ref, k_ref, v_ref, og_ref, gain_ref, conv_ref, corr_ref, row_ref,
    out_ref, gq_ref, gk_ref, gv_ref, gres_ref, grate_ref, gskip_ref,
):
    f32, bf16 = jnp.float32, jnp.bfloat16
    modes = gres_ref.shape[1]
    gain = column(gain_ref[...])
    q, k = q_ref[...].astype(f32), k_ref[...].astype(f32)
    v, og = v_ref[...].astype(f32), og_ref[...].astype(f32)
    mixed = (k * v).astype(bf16).astype(f32)
    gated = (og * q).astype(bf16).astype(f32)
    forward_sum = conv_ref[...].astype(f32) + gain * mixed
    input_grad = corr_ref[...].astype(f32) + gain * gated
    out_ref[...] = (q * forward_sum).astype(bf16)
    gq_ref[...] = (og * forward_sum).astype(bf16)
    gk_ref[...] = (input_grad * v).astype(bf16)
    gv_ref[...] = (input_grad * k).astype(bf16)
    gres_ref[...] = row_ref[:, 0:modes]
    grate_ref[...] = row_ref[:, modes : 2 * modes]
    gskip_ref[...] = row_ref[:, 2 * modes : 2 * modes + 1]


def body(queries, key_branch, value_branch, out_grad, residue, log_rate, skip_gain):
    sub = lax.axis_size("sub")
    devices = lax.axis_size("ctx") * sub
    channels, width = queries.shape
    modes = residue.shape[1]
    slab = 2 * width // LANES
    f32, bf16 = jnp.float32, jnp.bfloat16
    vmem = pl.BlockSpec(memory_space=pltpu.VMEM)
    wide = jax.ShapeDtypeStruct((channels, width), bf16)
    gain_row = jax.ShapeDtypeStruct((1, LANES), f32)
    hbm = pl.BlockSpec(memory_space=pltpu.HBM)
    conv, corr, row, *loaded = pl.pallas_call(
        functools.partial(exchange_kernel, devices, sub),
        out_shape=(wide, wide, gain_row, wide, wide, wide, wide, gain_row),
        in_specs=[hbm] * 7,
        out_specs=(vmem,) * 8,
        scratch_shapes=[
            pltpu.VMEM((1, modes), f32),
            pltpu.VMEM((1, modes), f32),
            pltpu.VMEM((channels * slab, LANES), f32),
            pltpu.VMEM((width, width), bf16),
            pltpu.VMEM((channels, slab, LANES), bf16),
            pltpu.VMEM((devices, slab, LANES), bf16),
            pltpu.VMEM((devices, slab, LANES), bf16),
            pltpu.VMEM((channels, slab, LANES), bf16),
            pltpu.SemaphoreType.DMA((7,)),
            pltpu.SemaphoreType.DMA,
            pltpu.SemaphoreType.DMA,
            pltpu.SemaphoreType.DMA,
            pltpu.SemaphoreType.DMA,
        ],
        compiler_params=pltpu.CompilerParams(
            collective_id=0, has_side_effects=True, vmem_limit_bytes=32 * 2**20
        ),
        name="exchange",
    )(*[pltpu.with_memory_space_constraint(x, pltpu.HBM) for x in (queries, key_branch, value_branch, out_grad, residue, log_rate, skip_gain[None, :])])
    output, grad_query, grad_key, grad_value, grad_residue, grad_rate, grad_skip = pl.pallas_call(
        finish_kernel,
        out_shape=(wide,) * 4
        + (jax.ShapeDtypeStruct((1, modes), f32),) * 2
        + (jax.ShapeDtypeStruct((1, 1), f32),),
        in_specs=[vmem] * 8,
        out_specs=(vmem,) * 7,
        compiler_params=pltpu.CompilerParams(vmem_limit_bytes=32 * 2**20),
        name="finish",
    )(*loaded, conv, corr, row)
    return (
        output, grad_query, grad_key, grad_value, grad_residue, grad_rate, grad_skip.reshape(1)
    )


def solution(mesh):
    wide = P(None, ("ctx", "sub"))
    rows = P(("ctx", "sub"), None)
    return jax.shard_map(
        body,
        mesh=mesh,
        in_specs=(wide, wide, wide, wide, rows, rows, P()),
        out_specs=(wide, wide, wide, wide, rows, rows, P(("ctx", "sub"))),
        check_vma=False,
    )
```

```python
import functools

import jax
import jax.numpy as jnp
from jax import lax
from jax.experimental import pallas as pl
from jax.experimental.pallas import tpu as pltpu
from jax.sharding import PartitionSpec as P

MESH = pl.DeviceIdType.MESH
FULL = lax.Precision.HIGHEST
NT = (((1,), (1,)), ((), ()))
TN = (((0,), (0,)), ((), ()))
LANES = 128
GROUPS = 8


def iota(shape, axis):
    return lax.broadcasted_iota(jnp.int32, shape, axis)


def column(row):
    n = row.shape[1]
    eye = iota((n, n), 0) == iota((n, n), 1)
    return jnp.sum(jnp.where(eye, row, 0.0), axis=1, keepdims=True)


def shifted(rows, count):
    n = rows.shape[0]
    if count > 0:
        moved = pltpu.roll(rows, count, 0)
        return jnp.where(iota(rows.shape, 0) >= count, moved, 0.0)
    moved = pltpu.roll(rows, n + count, 0)
    return jnp.where(iota(rows.shape, 0) < n + count, moved, 0.0)


def running(rows, speed, span, sign):
    n = rows.shape[0]
    step = 1
    while step < n:
        rows = rows + jnp.exp(-speed * float(span * step)) * shifted(rows, sign * step)
        step *= 2
    return shifted(rows, sign)


def partners(me):
    core, z = me % 2, me // 4 % 4
    y, x = me // 2 % 2 * 2 + me // 16 % 2, me // 32
    across = [lax.rem(x + d, 4) * 8 for d in range(4)]
    along = [lax.rem(z + d, 4) for d in range(4)]
    ups = [lax.rem(y + d, 4) for d in range(4)]
    high = [[u // 2 * 2 + lax.rem(core + d, 2) for d in range(2)] for u in ups]
    low = [lax.rem(u, 2) * 4 for u in ups]
    moves = [
        (dx, dy, dz, dc)
        for dx in range(4) for dy in range(4) for dz in range(4) for dc in range(2)
        if (dx, dy, dz, dc) != (0, 0, 0, 0)
    ]
    moves.sort(key=lambda m: -sum(min(d, 4 - d) for d in m[:3]))
    found = []
    for dx, dy, dz, dc in moves:
        ctx, sub = across[dx] + low[dy] + along[dz], high[dy][dc]
        found.append((ctx * 4 + sub, (ctx, sub)))
    return found


def send_all(peers, me, src, dst, send_sem, recv_sem):
    for peer, place in peers:
        row = 0 if src.shape[0] == 1 else peer
        pltpu.make_async_remote_copy(
            src_ref=src.at[pl.ds(row, 1)],
            dst_ref=dst.at[pl.ds(me, 1)],
            send_sem=send_sem,
            recv_sem=recv_sem,
            device_id=place,
            device_id_type=MESH,
        ).start()


def whole(peers, dst, send_sem, recv_sem):
    return pltpu.make_async_remote_copy(
        src_ref=dst.at[pl.ds(0, len(peers))],
        dst_ref=dst.at[pl.ds(0, len(peers))],
        send_sem=send_sem,
        recv_sem=recv_sem,
        device_id=peers[0][1],
        device_id_type=MESH,
    )


def loop_steps(count, unroll, step, carry):
    def some(i, carry):
        for j in range(unroll):
            carry = step(i * unroll + j, carry)
        return carry

    return lax.fori_loop(0, count // unroll, some, carry)


def tile_rows(step):
    return pl.ds(pl.multiple_of(step * GROUPS, GROUPS), GROUPS)


def scan_groups(x_ref, y_ref, steps, decays, gains, backward):
    def step(i, states):
        rows = tile_rows(steps - 1 - i if backward else i)
        x = x_ref[rows, :]
        states = [a * h + x for a, h in zip(decays, states)]
        y_ref[rows, :] = sum(g * h for g, h in zip(gains, states))
        return states

    start = [jnp.zeros((GROUPS, LANES), jnp.float32)] * len(decays)
    return loop_steps(steps, 4, step, start)


def add_states(y_ref, steps, decays, states, backward):
    def step(i, states):
        rows = tile_rows(steps - 1 - i if backward else i)
        states = [a * s for a, s in zip(decays, states)]
        y_ref[rows, :] = y_ref[rows, :] + sum(states)
        return states

    loop_steps(steps, 8, step, states)


def exchange_kernel(
    devices, sub, q_hbm, k_hbm, v_hbm, og_hbm, res_hbm, rate_hbm, gain_hbm,
    conv_ref, corr_ref, row_ref, q_ref, k_ref, v_ref, og_ref, gain_ref,
    res_ref, rate_ref, stage, out_buf, in_buf, par_buf, par_all, state_buf, state_all,
    mixed_t, gated_t, conv_t, corr_t, inner, powers,
    load_sems, out_send, out_recv, par_send, par_recv, state_send, state_recv,
):
    me = lax.axis_index("ctx") * sub + lax.axis_index("sub")
    channels, width = q_ref.shape
    blocks = width // LANES
    steps = width // GROUPS
    slab = 2 * blocks
    modes = res_ref.shape[1]
    f32, bf16 = jnp.float32, jnp.bfloat16
    peers = partners(me)
    barrier = pltpu.get_barrier_semaphore()
    for _, place in peers:
        pl.semaphore_signal(barrier, inc=1, device_id=place, device_id_type=MESH)
    loads = [
        pltpu.make_async_copy(src, dst, load_sems.at[i])
        for i, (src, dst) in enumerate(
            [(k_hbm, k_ref), (v_hbm, v_ref), (og_hbm, og_ref), (q_hbm, q_ref),
             (res_hbm, res_ref), (rate_hbm, rate_ref), (gain_hbm, gain_ref)]
        )
    ]
    for load in loads:
        load.start()
    for load in loads:
        load.wait()

    mixed_own = k_ref[...].astype(f32) * v_ref[...].astype(f32)
    gated_own = og_ref[...].astype(f32) * q_ref[...].astype(f32)
    for j in range(blocks):
        cols = slice(j * LANES, (j + 1) * LANES)
        stage[pl.ds(j, channels, stride=slab), :] = mixed_own[:, cols]
        stage[pl.ds(blocks + j, channels, stride=slab), :] = gated_own[:, cols]
    out_buf[...] = stage[...].astype(bf16).reshape(channels, slab, LANES)
    speed_row = jnp.exp(rate_ref[...])
    res_row = res_ref[...]
    par_buf[...] = jnp.zeros((1, LANES), f32)
    par_buf[:, 0:modes] = speed_row
    par_buf[:, modes : 2 * modes] = res_row

    pl.semaphore_wait(barrier, devices - 1)
    send_all(peers, me, out_buf, in_buf, out_send, out_recv)
    send_all(peers, me, par_buf, par_all, par_send, par_recv)
    in_buf[me] = out_buf[me]
    par_all[pl.ds(me, 1), :] = par_buf[...]

    speed = column(speed_row)
    pos = iota((modes, width), 1).astype(f32)
    rise = jnp.exp(-speed * pos)
    fall = jnp.exp(-speed * (width - 1.0 - pos))
    to_end = fall.astype(bf16)
    to_end_timed = (fall * (width - 1.0 - pos)).astype(bf16)
    to_start = rise.astype(bf16)
    to_start_timed = (rise * pos).astype(bf16)
    grow = jnp.exp(speed * iota((modes, LANES), 1).astype(f32))
    mixed_own = (k_ref[...].astype(f32) * v_ref[...].astype(f32)).astype(bf16).astype(f32)
    gated_own = (og_ref[...].astype(f32) * q_ref[...].astype(f32)).astype(bf16).astype(f32)
    per_block = LANES // steps
    for own, turned in ((mixed_own, mixed_t), (gated_own, gated_t)):
        for j in range(blocks):
            block = own[:, j * LANES : (j + 1) * LANES].T
            for g in range(per_block):
                turned[pl.ds(j * per_block + g, steps, stride=GROUPS), :] = block[
                    g * steps : (g + 1) * steps, :
                ]

    whole(peers, in_buf, out_send, out_recv).wait_recv()
    stage[...] = in_buf[...].reshape(devices * slab, LANES).astype(f32)

    def gathered(start):
        parts = [stage[pl.ds(start + j, devices, stride=slab), :] for j in range(blocks)]
        return jnp.concatenate(parts, axis=1).astype(bf16)

    mixed, gated = gathered(0), gathered(blocks)

    def state(rows, weights):
        return lax.dot_general(rows, weights, NT, preferred_element_type=f32)

    ends, starts = state(mixed, to_end), state(gated, to_start)
    before = running(ends, speed_row, width, 1)
    after = running(starts, speed_row, width, -1)
    state_buf[:, 0:modes] = before
    state_buf[:, modes : 2 * modes] = after
    send_all(peers, me, state_buf, state_all, state_send, state_recv)
    state_all[pl.ds(me, 1), :] = state_buf[pl.ds(me, 1), :]

    whole(peers, par_all, par_send, par_recv).wait_recv()
    params = par_all[...].T
    speeds = [jnp.broadcast_to(params[r : r + 1, :], (GROUPS, LANES)) for r in range(modes)]
    gains = [
        jnp.broadcast_to(params[modes + r : modes + r + 1, :], (GROUPS, LANES))
        for r in range(modes)
    ]
    decays = [jnp.exp(-x) for x in speeds]
    group = iota((GROUPS, LANES), 0)
    for backward, x_ref, y_ref in ((False, mixed_t, conv_t), (True, gated_t, corr_t)):
        found = scan_groups(x_ref, y_ref, steps, decays, gains, backward)
        for r in range(modes):
            sums = found[r]
            sign = -1 if backward else 1
            step = 1
            while step < GROUPS:
                sums = sums + jnp.exp(-speeds[r] * float(steps * step)) * shifted(sums, sign * step)
                step *= 2
            at = backward * modes + r
            inner[at] = gains[r] * shifted(sums, sign)
            away = (GROUPS - 1 - group) if backward else group
            powers[at] = gains[r] * jnp.exp(-speeds[r] * (away * steps).astype(f32))

    pairs = lax.dot_general(mixed, gated, TN, preferred_element_type=f32)
    lag = iota((LANES, width), 1) - iota((LANES, width), 0)
    lagged = []
    for k in range(blocks):
        total = pairs[:LANES, k * LANES : (k + 1) * LANES]
        for row in range(1, blocks - k):
            rows = slice(row * LANES, (row + 1) * LANES)
            total = total + pairs[rows, (row + k) * LANES : (row + k + 1) * LANES]
        lagged.append(total)
    lagged = jnp.where(lag >= 0, jnp.concatenate(lagged, axis=1), 0.0)
    skip_sum = jnp.sum(jnp.where(lag == 0, lagged, 0.0), keepdims=True)

    def local_sum(values):
        by_lag = jnp.dot(grow, values, precision=FULL, preferred_element_type=f32)
        return jnp.sum(by_lag * rise, axis=1, keepdims=True)

    plain_col = local_sum(lagged)
    timed_col = local_sum(lagged * lag.astype(f32))
    eye = iota((modes, modes), 0) == iota((modes, modes), 1)

    def as_row(col):
        return jnp.sum(jnp.where(eye, col, 0.0), axis=0, keepdims=True)

    one_step = jnp.exp(-speed_row)
    chunk_step = jnp.exp(-speed_row * float(width))
    ends_timed, starts_timed = state(mixed, to_end_timed), state(gated, to_start_timed)
    cross = before * starts
    cross_timed = ends_timed * after + before * starts_timed + cross
    cross_timed = cross_timed + (float(width) * chunk_step) * (before * after)
    plain = as_row(plain_col) + one_step * jnp.sum(cross, axis=0, keepdims=True)
    timed = as_row(timed_col) + one_step * jnp.sum(cross_timed, axis=0, keepdims=True)
    seq_len = devices * width
    row_ref[0:1, :] = jnp.zeros((1, LANES), f32)
    row_ref[0:1, 0:modes] = plain * (1.0 / seq_len)
    row_ref[0:1, modes : 2 * modes] = -res_row * speed_row * timed * (1.0 / seq_len**0.5)
    row_ref[0:1, 2 * modes : 2 * modes + 1] = skip_sum

    whole(peers, state_all, state_send, state_recv).wait_recv()
    states = state_all[...].T
    for backward, y_ref, to_ref in ((False, conv_t, conv_ref), (True, corr_t, corr_ref)):
        start = []
        for r in range(modes):
            at = backward * modes + r
            start.append(inner[at] + powers[at] * states[at : at + 1, :])
        add_states(y_ref, steps, decays, start, backward)
        for j in range(blocks):
            parts = [
                y_ref[pl.ds(j * per_block + g, steps, stride=GROUPS), :] for g in range(per_block)
            ]
            to_ref[:, j * LANES : (j + 1) * LANES] = jnp.concatenate(parts, axis=0).T
    whole(peers, in_buf, out_send, out_recv).wait_send()
    whole(peers, par_all, par_send, par_recv).wait_send()
    whole(peers, state_all, state_send, state_recv).wait_send()


def finish_kernel(
    q_ref, k_ref, v_ref, og_ref, gain_ref, conv_ref, corr_ref, row_ref,
    out_ref, gq_ref, gk_ref, gv_ref, gres_ref, grate_ref, gskip_ref,
):
    f32, bf16 = jnp.float32, jnp.bfloat16
    modes = gres_ref.shape[1]
    gain = column(gain_ref[...])
    q, k = q_ref[...].astype(f32), k_ref[...].astype(f32)
    v, og = v_ref[...].astype(f32), og_ref[...].astype(f32)
    mixed = (k * v).astype(bf16).astype(f32)
    gated = (og * q).astype(bf16).astype(f32)
    forward_sum = conv_ref[...] + gain * mixed
    input_grad = corr_ref[...] + gain * gated
    out_ref[...] = (q * forward_sum).astype(bf16)
    gq_ref[...] = (og * forward_sum).astype(bf16)
    gk_ref[...] = (input_grad * v).astype(bf16)
    gv_ref[...] = (input_grad * k).astype(bf16)
    gres_ref[...] = row_ref[:, 0:modes]
    grate_ref[...] = row_ref[:, modes : 2 * modes]
    gskip_ref[...] = row_ref[:, 2 * modes : 2 * modes + 1]


def body(queries, key_branch, value_branch, out_grad, residue, log_rate, skip_gain):
    sub = lax.axis_size("sub")
    devices = lax.axis_size("ctx") * sub
    channels, width = queries.shape
    modes = residue.shape[1]
    slab = 2 * width // LANES
    f32, bf16 = jnp.float32, jnp.bfloat16
    vmem = pl.BlockSpec(memory_space=pltpu.VMEM)
    wide = jax.ShapeDtypeStruct((channels, width), bf16)
    full = jax.ShapeDtypeStruct((channels, width), f32)
    gain_row = jax.ShapeDtypeStruct((1, LANES), f32)
    hbm = pl.BlockSpec(memory_space=pltpu.HBM)
    conv, corr, row, *loaded = pl.pallas_call(
        functools.partial(exchange_kernel, devices, sub),
        out_shape=(full, full, gain_row, wide, wide, wide, wide, gain_row),
        in_specs=[hbm] * 7,
        out_specs=(vmem,) * 8,
        scratch_shapes=[
            pltpu.VMEM((1, modes), f32),
            pltpu.VMEM((1, modes), f32),
            pltpu.VMEM((channels * slab, LANES), f32),
            pltpu.VMEM((channels, slab, LANES), bf16),
            pltpu.VMEM((devices, slab, LANES), bf16),
            pltpu.VMEM((1, LANES), f32),
            pltpu.VMEM((channels, LANES), f32),
            pltpu.VMEM((devices, LANES), f32),
            pltpu.VMEM((channels, LANES), f32),
            pltpu.VMEM((width, LANES), f32),
            pltpu.VMEM((width, LANES), f32),
            pltpu.VMEM((width, LANES), f32),
            pltpu.VMEM((width, LANES), f32),
            pltpu.VMEM((2 * modes, GROUPS, LANES), f32),
            pltpu.VMEM((2 * modes, GROUPS, LANES), f32),
            pltpu.SemaphoreType.DMA((7,)),
            pltpu.SemaphoreType.DMA,
            pltpu.SemaphoreType.DMA,
            pltpu.SemaphoreType.DMA,
            pltpu.SemaphoreType.DMA,
            pltpu.SemaphoreType.DMA,
            pltpu.SemaphoreType.DMA,
        ],
        compiler_params=pltpu.CompilerParams(
            collective_id=0, has_side_effects=True, vmem_limit_bytes=32 * 2**20
        ),
        name="exchange",
    )(*[pltpu.with_memory_space_constraint(x, pltpu.HBM) for x in (queries, key_branch, value_branch, out_grad, residue, log_rate, skip_gain[None, :])])
    output, grad_query, grad_key, grad_value, grad_residue, grad_rate, grad_skip = pl.pallas_call(
        finish_kernel,
        out_shape=(wide,) * 4
        + (jax.ShapeDtypeStruct((1, modes), f32),) * 2
        + (jax.ShapeDtypeStruct((1, 1), f32),),
        in_specs=[vmem] * 8,
        out_specs=(vmem,) * 7,
        compiler_params=pltpu.CompilerParams(vmem_limit_bytes=32 * 2**20),
        name="finish",
    )(*loaded, conv, corr, row)
    return (
        output, grad_query, grad_key, grad_value, grad_residue, grad_rate, grad_skip.reshape(1)
    )


def solution(mesh):
    wide = P(None, ("ctx", "sub"))
    rows = P(("ctx", "sub"), None)
    return jax.shard_map(
        body,
        mesh=mesh,
        in_specs=(wide, wide, wide, wide, rows, rows, P()),
        out_specs=(wide, wide, wide, wide, rows, rows, P(("ctx", "sub"))),
        check_vma=False,
    )
```

```python
import functools

import jax
import jax.numpy as jnp
from jax import lax
from jax.experimental import pallas as pl
from jax.experimental.pallas import tpu as pltpu
from jax.sharding import PartitionSpec as P

MESH = pl.DeviceIdType.MESH
FULL = lax.Precision.HIGHEST
NT = (((1,), (1,)), ((), ()))
TN = (((0,), (0,)), ((), ()))
LANES = 128
GROUPS = 8


def iota(shape, axis):
    return lax.broadcasted_iota(jnp.int32, shape, axis)


def column(row):
    n = row.shape[1]
    eye = iota((n, n), 0) == iota((n, n), 1)
    return jnp.sum(jnp.where(eye, row, 0.0), axis=1, keepdims=True)


def as_row(col):
    n = col.shape[0]
    eye = iota((n, n), 0) == iota((n, n), 1)
    return jnp.sum(jnp.where(eye, col, 0.0), axis=0, keepdims=True)


def shifted(rows, count):
    n = rows.shape[0]
    if count > 0:
        moved = pltpu.roll(rows, count, 0)
        return jnp.where(iota(rows.shape, 0) >= count, moved, 0.0)
    moved = pltpu.roll(rows, n + count, 0)
    return jnp.where(iota(rows.shape, 0) < n + count, moved, 0.0)


def running(rows, speed, span, sign):
    n = rows.shape[0]
    step = 1
    while step < n:
        rows = rows + jnp.exp(-speed * float(span * step)) * shifted(rows, sign * step)
        step *= 2
    return shifted(rows, sign)


def partners(me):
    core, z = me % 2, me // 4 % 4
    y, x = me // 2 % 2 * 2 + me // 16 % 2, me // 32
    across = [lax.rem(x + d, 4) * 8 for d in range(4)]
    along = [lax.rem(z + d, 4) for d in range(4)]
    ups = [lax.rem(y + d, 4) for d in range(4)]
    high = [[u // 2 * 2 + lax.rem(core + d, 2) for d in range(2)] for u in ups]
    low = [lax.rem(u, 2) * 4 for u in ups]
    moves = [
        (dx, dy, dz, dc)
        for dx in range(4) for dy in range(4) for dz in range(4) for dc in range(2)
        if (dx, dy, dz, dc) != (0, 0, 0, 0)
    ]
    moves.sort(key=lambda m: -sum(min(d, 4 - d) for d in m[:3]))
    found = []
    for dx, dy, dz, dc in moves:
        ctx, sub = across[dx] + low[dy] + along[dz], high[dy][dc]
        found.append((ctx * 4 + sub, (ctx, sub)))
    return found


def send_all(peers, me, src, dst, send_sem, recv_sem):
    for peer, place in peers:
        row = 0 if src.shape[0] == 1 else peer
        pltpu.make_async_remote_copy(
            src_ref=src.at[pl.ds(row, 1)],
            dst_ref=dst.at[pl.ds(me, 1)],
            send_sem=send_sem,
            recv_sem=recv_sem,
            device_id=place,
            device_id_type=MESH,
        ).start()


def whole(peers, dst, send_sem, recv_sem):
    return pltpu.make_async_remote_copy(
        src_ref=dst.at[pl.ds(0, len(peers))],
        dst_ref=dst.at[pl.ds(0, len(peers))],
        send_sem=send_sem,
        recv_sem=recv_sem,
        device_id=peers[0][1],
        device_id_type=MESH,
    )


def loop_steps(count, unroll, step, carry):
    def some(i, carry):
        for j in range(unroll):
            carry = step(i * unroll + j, carry)
        return carry

    return lax.fori_loop(0, count // unroll, some, carry)


def tile_rows(step):
    return pl.ds(pl.multiple_of(step * GROUPS, GROUPS), GROUPS)


def scan_groups(x_ref, y_ref, steps, decays, gains, backward):
    def step(i, states):
        rows = tile_rows(steps - 1 - i if backward else i)
        x = x_ref[rows, :]
        states = [a * h + x for a, h in zip(decays, states)]
        y_ref[rows, :] = sum(g * h for g, h in zip(gains, states))
        return states

    start = [jnp.zeros((GROUPS, LANES), jnp.float32)] * len(decays)
    return loop_steps(steps, 4, step, start)


def add_states(y_ref, steps, decays, states, backward):
    def step(i, states):
        rows = tile_rows(steps - 1 - i if backward else i)
        states = [a * s for a, s in zip(decays, states)]
        y_ref[rows, :] = y_ref[rows, :] + sum(states)
        return states

    loop_steps(steps, 8, step, states)


def natural(y_ref, steps, j):
    per_block = LANES // steps
    parts = [
        y_ref[pl.ds(j * per_block + g, steps, stride=GROUPS), :] for g in range(per_block)
    ]
    return jnp.concatenate(parts, axis=0).T


def exchange_kernel(
    devices, sub, q_hbm, k_hbm, v_hbm, og_hbm, res_hbm, rate_hbm, gain_hbm,
    sum_ref, grad_ref, row_ref, q_ref, k_ref, v_ref, og_ref, state_ref, factor_ref, rise_ref,
    fall_ref, gain_ref, res_ref, rate_ref, stage, out_buf, in_buf, par_buf, par_all, state_buf, state_all,
    mixed_t, gated_t, conv_t, corr_t,
    load_sems, out_send, out_recv, par_send, par_recv, state_send, state_recv,
):
    me = lax.axis_index("ctx") * sub + lax.axis_index("sub")
    channels, width = q_ref.shape
    blocks = width // LANES
    steps = width // GROUPS
    slab = 2 * blocks
    modes = res_ref.shape[1]
    f32, bf16 = jnp.float32, jnp.bfloat16
    peers = partners(me)
    barrier = pltpu.get_barrier_semaphore()
    for _, place in peers:
        pl.semaphore_signal(barrier, inc=1, device_id=place, device_id_type=MESH)
    loads = [
        pltpu.make_async_copy(src, dst, load_sems.at[i])
        for i, (src, dst) in enumerate(
            [(k_hbm, k_ref), (v_hbm, v_ref), (og_hbm, og_ref), (q_hbm, q_ref),
             (res_hbm, res_ref), (rate_hbm, rate_ref), (gain_hbm, gain_ref)]
        )
    ]
    for load in loads:
        load.start()
    for load in loads:
        load.wait()

    mixed_own = k_ref[...].astype(f32) * v_ref[...].astype(f32)
    gated_own = og_ref[...].astype(f32) * q_ref[...].astype(f32)
    for j in range(blocks):
        cols = slice(j * LANES, (j + 1) * LANES)
        stage[pl.ds(j, channels, stride=slab), :] = mixed_own[:, cols]
        stage[pl.ds(blocks + j, channels, stride=slab), :] = gated_own[:, cols]
    out_buf[...] = stage[...].astype(bf16).reshape(channels, slab, LANES)
    speed_row = jnp.exp(rate_ref[...])
    res_row = res_ref[...]
    par_buf[...] = jnp.zeros((1, LANES), f32)
    par_buf[:, 0:modes] = speed_row
    par_buf[:, modes : 2 * modes] = res_row

    pl.semaphore_wait(barrier, devices - 1)
    send_all(peers, me, out_buf, in_buf, out_send, out_recv)
    send_all(peers, me, par_buf, par_all, par_send, par_recv)
    in_buf[me] = out_buf[me]
    par_all[pl.ds(me, 1), :] = par_buf[...]

    speed = column(speed_row)
    copies = LANES // modes
    half = copies // 2
    wide_speed = as_row(jnp.concatenate([speed] * copies, axis=0))
    pos = iota((modes, width), 1).astype(f32)
    rise = jnp.exp(-speed * pos)
    fall = jnp.exp(-speed * (width - 1.0 - pos))
    blank = jnp.zeros((half * modes, width), f32)
    to_end = jnp.concatenate([fall] * half + [blank], axis=0).astype(bf16)
    to_start = jnp.concatenate([blank] + [rise] * half, axis=0).astype(bf16)
    to_end_timed = (fall * (width - 1.0 - pos)).astype(bf16)
    to_start_timed = (rise * pos).astype(bf16)
    grow = jnp.exp(speed * iota((modes, LANES), 1).astype(f32))
    mixed_own = (k_ref[...].astype(f32) * v_ref[...].astype(f32)).astype(bf16).astype(f32)
    gated_own = (og_ref[...].astype(f32) * q_ref[...].astype(f32)).astype(bf16).astype(f32)
    per_block = LANES // steps
    for own, turned in ((mixed_own, mixed_t), (gated_own, gated_t)):
        for j in range(blocks):
            block = own[:, j * LANES : (j + 1) * LANES].T
            for g in range(per_block):
                turned[pl.ds(j * per_block + g, steps, stride=GROUPS), :] = block[
                    g * steps : (g + 1) * steps, :
                ]

    whole(peers, in_buf, out_send, out_recv).wait_recv()
    stage[...] = in_buf[...].reshape(devices * slab, LANES).astype(f32)

    def gathered(start):
        parts = [stage[pl.ds(start + j, devices, stride=slab), :] for j in range(blocks)]
        return jnp.concatenate(parts, axis=1).astype(bf16)

    mixed, gated = gathered(0), gathered(blocks)

    def state(rows, weights):
        return lax.dot_general(rows, weights, NT, preferred_element_type=f32)

    ends, starts = state(mixed, to_end), state(gated, to_start)
    before = running(ends, wide_speed, width, 1)
    after = running(starts, wide_speed, width, -1)
    state_buf[...] = before + after
    send_all(peers, me, state_buf, state_all, state_send, state_recv)
    state_all[pl.ds(me, 1), :] = state_buf[pl.ds(me, 1), :]

    whole(peers, par_all, par_send, par_recv).wait_recv()
    params = par_all[...].T
    speeds = [jnp.broadcast_to(params[r : r + 1, :], (GROUPS, LANES)) for r in range(modes)]
    gains = [
        jnp.broadcast_to(params[modes + r : modes + r + 1, :], (GROUPS, LANES))
        for r in range(modes)
    ]
    decays = [jnp.exp(-x) for x in speeds]
    gain = column(gain_ref[...])
    for backward, own, x_ref, y_ref, to_ref in (
        (False, mixed_own, mixed_t, conv_t, sum_ref), (True, gated_own, gated_t, corr_t, grad_ref)
    ):
        found = scan_groups(x_ref, y_ref, steps, decays, gains, backward)
        sign = -1 if backward else 1
        inner = []
        for r in range(modes):
            sums = found[r]
            step = 1
            while step < GROUPS:
                sums = sums + jnp.exp(-speeds[r] * float(steps * step)) * shifted(sums, sign * step)
                step *= 2
            inner.append(gains[r] * shifted(sums, sign))
        add_states(y_ref, steps, decays, inner, backward)
        for j in range(blocks):
            cols = slice(j * LANES, (j + 1) * LANES)
            to_ref[:, cols] = natural(y_ref, steps, j) + gain * own[:, cols]

    lane = iota((channels, LANES), 1)
    own_gain = jnp.where((lane >= modes) & (lane < 2 * modes), par_all[...], 0.0)
    own_gain = pltpu.roll(own_gain, LANES - modes, 1)
    own_speed = jnp.where(lane < modes, par_all[...], 0.0)
    step = modes
    while step < LANES:
        own_gain = own_gain + pltpu.roll(own_gain, step, 1)
        own_speed = own_speed + pltpu.roll(own_speed, step, 1)
        step *= 2
    home = iota((channels, LANES), 0) % (2 * copies) - lane // modes
    for n in range(blocks):
        scaled = own_gain * jnp.exp(-own_speed * float(n * LANES))
        factor_ref[n, :, :LANES] = jnp.where(home == 0, scaled, 0.0)
        factor_ref[n, :, LANES:] = jnp.where(home == copies, scaled, 0.0)
    ahead = (iota((modes, LANES), 1) + 1).astype(f32)
    behind = (LANES - iota((modes, LANES), 1)).astype(f32)
    for c in range(channels):
        rate = -params[:modes, c : c + 1]
        rows = slice(c * modes, (c + 1) * modes)
        rise_ref[rows, :] = jnp.exp(rate * ahead).astype(bf16)
        fall_ref[rows, :] = jnp.exp(rate * behind).astype(bf16)

    pairs = lax.dot_general(mixed, gated, TN, preferred_element_type=f32)
    lag = iota((LANES, width), 1) - iota((LANES, width), 0)
    lagged = []
    for k in range(blocks):
        total = pairs[:LANES, k * LANES : (k + 1) * LANES]
        for row in range(1, blocks - k):
            rows = slice(row * LANES, (row + 1) * LANES)
            total = total + pairs[rows, (row + k) * LANES : (row + k + 1) * LANES]
        lagged.append(total)
    lagged = jnp.where(lag >= 0, jnp.concatenate(lagged, axis=1), 0.0)
    skip_sum = jnp.sum(jnp.where(lag == 0, lagged, 0.0), keepdims=True)

    def local_sum(values):
        by_lag = jnp.dot(grow, values, precision=FULL, preferred_element_type=f32)
        return jnp.sum(by_lag * rise, axis=1, keepdims=True)

    plain_col = local_sum(lagged)
    timed_col = local_sum(lagged * lag.astype(f32))
    one_step = jnp.exp(-speed_row)
    chunk_step = jnp.exp(-speed_row * float(width))
    ends_timed, starts_timed = state(mixed, to_end_timed), state(gated, to_start_timed)
    first, second = slice(0, modes), slice(half * modes, (half + 1) * modes)
    before, after, starts = before[:, first], after[:, second], starts[:, second]
    cross = before * starts
    cross_timed = ends_timed * after + before * starts_timed + cross
    cross_timed = cross_timed + (float(width) * chunk_step) * (before * after)
    plain = as_row(plain_col) + one_step * jnp.sum(cross, axis=0, keepdims=True)
    timed = as_row(timed_col) + one_step * jnp.sum(cross_timed, axis=0, keepdims=True)
    seq_len = devices * width
    row_ref[0:1, :] = jnp.zeros((1, LANES), f32)
    row_ref[0:1, 0:modes] = plain * (1.0 / seq_len)
    row_ref[0:1, modes : 2 * modes] = -res_row * speed_row * timed * (1.0 / seq_len**0.5)
    row_ref[0:1, 2 * modes : 2 * modes + 1] = skip_sum

    whole(peers, in_buf, out_send, out_recv).wait_send()
    whole(peers, par_all, par_send, par_recv).wait_send()
    whole(peers, state_all, state_send, state_recv).wait_recv()
    state_ref[...] = state_all[...]
    whole(peers, state_all, state_send, state_recv).wait_send()


def finish_kernel(
    q_ref, k_ref, v_ref, og_ref, sum_ref, grad_ref, row_ref, state_ref, factor_ref, rise_ref,
    fall_ref, out_ref, gq_ref, gk_ref, gv_ref, gres_ref, grate_ref, gskip_ref,
):
    f32, bf16 = jnp.float32, jnp.bfloat16
    channels, width = q_ref.shape
    modes = gres_ref.shape[1]
    copies = LANES // modes
    gres_ref[...] = row_ref[:, 0:modes]
    grate_ref[...] = row_ref[:, modes : 2 * modes]
    gskip_ref[...] = row_ref[:, 2 * modes : 2 * modes + 1]
    blocks = width // LANES
    tall = 2 * copies
    states = state_ref[...]
    other = pltpu.roll(states, LANES // 2, 1)
    first = iota((channels, LANES), 1) < LANES // 2
    before = jnp.where(first, states, other)
    after = jnp.where(first, other, states)
    for g in range(channels // tall):
        rows = slice(g * tall, (g + 1) * tall)
        deep = slice(g * tall * modes, (g + 1) * tall * modes)
        for found, order, table_ref, base_ref, pair, places in (
            (before, 1, rise_ref, sum_ref, (q_ref, og_ref), (out_ref, gq_ref)),
            (after, -1, fall_ref, grad_ref, (v_ref, k_ref), (gk_ref, gv_ref)),
        ):
            own = jnp.concatenate([found[rows, :]] * 2, axis=1)
            parts = [own * factor_ref[n, rows, :] for n in range(blocks)][::order]
            share = jnp.dot(
                jnp.concatenate(parts, axis=0).astype(bf16),
                table_ref[deep, :],
                preferred_element_type=f32,
            )
            for n in range(blocks):
                cols = slice(n * LANES, (n + 1) * LANES)
                total = share[n * tall : (n + 1) * tall, :] + base_ref[rows, cols]
                for factor, place in zip(pair, places):
                    place[rows, cols] = (factor[rows, cols].astype(f32) * total).astype(bf16)


def body(queries, key_branch, value_branch, out_grad, residue, log_rate, skip_gain):
    sub = lax.axis_size("sub")
    devices = lax.axis_size("ctx") * sub
    channels, width = queries.shape
    modes = residue.shape[1]
    slab = 2 * width // LANES
    f32, bf16 = jnp.float32, jnp.bfloat16
    vmem = pl.BlockSpec(memory_space=pltpu.VMEM)
    wide = jax.ShapeDtypeStruct((channels, width), bf16)
    full = jax.ShapeDtypeStruct((channels, width), f32)
    square = jax.ShapeDtypeStruct((channels, LANES), f32)
    table = jax.ShapeDtypeStruct((channels * modes, LANES), bf16)
    factors = jax.ShapeDtypeStruct((width // LANES, channels, 2 * LANES), f32)
    hbm = pl.BlockSpec(memory_space=pltpu.HBM)
    operands = (queries, key_branch, value_branch, out_grad, residue, log_rate, skip_gain[None, :])
    total, grad, row, q, k, v, og, *states = pl.pallas_call(
        functools.partial(exchange_kernel, devices, sub),
        out_shape=(
            full, full, jax.ShapeDtypeStruct((1, LANES), f32), wide, wide, wide, wide,
            square, factors, table, table,
        ),
        in_specs=[hbm] * 7,
        out_specs=(vmem,) * 11,
        scratch_shapes=[
            pltpu.VMEM((1, channels), f32),
            pltpu.VMEM((1, modes), f32),
            pltpu.VMEM((1, modes), f32),
            pltpu.VMEM((channels * slab, LANES), f32),
            pltpu.VMEM((channels, slab, LANES), bf16),
            pltpu.VMEM((devices, slab, LANES), bf16),
            pltpu.VMEM((1, LANES), f32),
            pltpu.VMEM((channels, LANES), f32),
            pltpu.VMEM((devices, LANES), f32),
            pltpu.VMEM((channels, LANES), f32),
            pltpu.VMEM((width, LANES), f32),
            pltpu.VMEM((width, LANES), f32),
            pltpu.VMEM((width, LANES), f32),
            pltpu.VMEM((width, LANES), f32),
            pltpu.SemaphoreType.DMA((7,)),
            pltpu.SemaphoreType.DMA,
            pltpu.SemaphoreType.DMA,
            pltpu.SemaphoreType.DMA,
            pltpu.SemaphoreType.DMA,
            pltpu.SemaphoreType.DMA,
            pltpu.SemaphoreType.DMA,
        ],
        compiler_params=pltpu.CompilerParams(
            collective_id=0, has_side_effects=True, vmem_limit_bytes=32 * 2**20
        ),
        name="exchange",
    )(*[pltpu.with_memory_space_constraint(x, pltpu.HBM) for x in operands])
    output, grad_query, grad_key, grad_value, grad_residue, grad_rate, grad_skip = pl.pallas_call(
        finish_kernel,
        out_shape=(wide,) * 4
        + (jax.ShapeDtypeStruct((1, modes), f32),) * 2
        + (jax.ShapeDtypeStruct((1, 1), f32),),
        in_specs=[vmem] * 11,
        out_specs=(vmem,) * 7,
        compiler_params=pltpu.CompilerParams(vmem_limit_bytes=32 * 2**20),
        name="finish",
    )(q, k, v, og, total, grad, row, *states)
    return (
        output, grad_query, grad_key, grad_value, grad_residue, grad_rate, grad_skip.reshape(1)
    )


def solution(mesh):
    wide = P(None, ("ctx", "sub"))
    rows = P(("ctx", "sub"), None)
    return jax.shard_map(
        body,
        mesh=mesh,
        in_specs=(wide, wide, wide, wide, rows, rows, P()),
        out_specs=(wide, wide, wide, wide, rows, rows, P(("ctx", "sub"))),
        check_vma=False,
    )
```

```python
import functools

import jax
import jax.numpy as jnp
from jax import lax
from jax.experimental import pallas as pl
from jax.experimental.pallas import tpu as pltpu
from jax.sharding import PartitionSpec as P

MESH = pl.DeviceIdType.MESH
FULL = lax.Precision.HIGHEST
NT = (((1,), (1,)), ((), ()))
TN = (((0,), (0,)), ((), ()))
LANES = 128
GROUPS = 8
FAR = (
    (2, 2, 2), (2, 2, 1), (2, 2, 3), (2, 1, 2), (2, 3, 2), (1, 2, 2), (3, 2, 2), (2, 3, 3), (3, 2, 3)
)


def iota(shape, axis):
    return lax.broadcasted_iota(jnp.int32, shape, axis)


def column(row):
    n = row.shape[1]
    eye = iota((n, n), 0) == iota((n, n), 1)
    return jnp.sum(jnp.where(eye, row, 0.0), axis=1, keepdims=True)


def as_row(col):
    n = col.shape[0]
    eye = iota((n, n), 0) == iota((n, n), 1)
    return jnp.sum(jnp.where(eye, col, 0.0), axis=0, keepdims=True)


def shifted(rows, count):
    n = rows.shape[0]
    if count > 0:
        moved = pltpu.roll(rows, count, 0)
        return jnp.where(iota(rows.shape, 0) >= count, moved, 0.0)
    moved = pltpu.roll(rows, n + count, 0)
    return jnp.where(iota(rows.shape, 0) < n + count, moved, 0.0)


def running(rows, speed, span, sign):
    n = rows.shape[0]
    step = 1
    while step < n:
        rows = rows + jnp.exp(-speed * float(span * step)) * shifted(rows, sign * step)
        step *= 2
    return shifted(rows, sign)


def place_of(me):
    core, z = me % 2, me // 4 % 4
    y, x = me // 2 % 2 * 2 + me // 16 % 2, me // 32
    return x, y, z, core


def index_of(x, y, z, core):
    return x * 32 + y % 2 * 16 + z * 4 + y // 2 * 2 + core


def opposite(chip):
    return tuple((v + 2) % 4 for v in chip)


def among(place, chips):
    x, y, z, _ = place
    mine = x * 16 + y * 4 + z
    found = mine < 0
    for cx, cy, cz in chips:
        found = jnp.logical_or(found, mine == cx * 16 + cy * 4 + cz)
    return found


def partners(me):
    x, y, z, core = place_of(me)
    across = [lax.rem(x + d, 4) * 8 for d in range(4)]
    along = [lax.rem(z + d, 4) for d in range(4)]
    ups = [lax.rem(y + d, 4) for d in range(4)]
    high = [[u // 2 * 2 + lax.rem(core + d, 2) for d in range(2)] for u in ups]
    low = [lax.rem(u, 2) * 4 for u in ups]
    moves = [
        (dx, dy, dz, dc)
        for dx in range(4) for dy in range(4) for dz in range(4) for dc in range(2)
        if (dx, dy, dz, dc) != (0, 0, 0, 0)
    ]
    moves.sort(key=lambda m: -sum(min(d, 4 - d) for d in m[:3]))
    found = []
    for dx, dy, dz, dc in moves:
        ctx, sub = across[dx] + low[dy] + along[dz], high[dy][dc]
        found.append((ctx * 4 + sub, (ctx, sub)))
    return found


def row_copy(src, row, dst, at, send_sem, recv_sem, place):
    return pltpu.make_async_remote_copy(
        src_ref=src.at[pl.ds(row, 1)],
        dst_ref=dst.at[pl.ds(at, 1)],
        send_sem=send_sem,
        recv_sem=recv_sem,
        device_id=place,
        device_id_type=MESH,
    )


def send_all(peers, at, src, dst, send_sem, recv_sem):
    for peer, place in peers:
        row = 0 if src.shape[0] == 1 else peer
        row_copy(src, row, dst, at, send_sem, recv_sem, place).start()


def whole(peers, dst, send_sem, recv_sem, count=None):
    count = count or len(peers)
    return pltpu.make_async_remote_copy(
        src_ref=dst.at[pl.ds(0, count)],
        dst_ref=dst.at[pl.ds(0, count)],
        send_sem=send_sem,
        recv_sem=recv_sem,
        device_id=peers[0][1],
        device_id_type=MESH,
    )


def loop_steps(count, unroll, step, carry):
    def some(i, carry):
        for j in range(unroll):
            carry = step(i * unroll + j, carry)
        return carry

    return lax.fori_loop(0, count // unroll, some, carry)


def tile_rows(step):
    return pl.ds(pl.multiple_of(step * GROUPS, GROUPS), GROUPS)


def scan_groups(x_ref, y_ref, steps, decays, gains, backward):
    def step(i, states):
        rows = tile_rows(steps - 1 - i if backward else i)
        x = x_ref[rows, :]
        states = [a * h + x for a, h in zip(decays, states)]
        y_ref[rows, :] = sum(g * h for g, h in zip(gains, states))
        return states

    start = [jnp.zeros((GROUPS, LANES), jnp.float32)] * len(decays)
    return loop_steps(steps, 4, step, start)


def add_states(y_ref, steps, decays, states, backward):
    def step(i, states):
        rows = tile_rows(steps - 1 - i if backward else i)
        states = [a * s for a, s in zip(decays, states)]
        y_ref[rows, :] = y_ref[rows, :] + sum(states)
        return states

    loop_steps(steps, 8, step, states)


def natural(y_ref, steps, j):
    per_block = LANES // steps
    parts = [
        y_ref[pl.ds(j * per_block + g, steps, stride=GROUPS), :] for g in range(per_block)
    ]
    return jnp.concatenate(parts, axis=0).T


def exchange_kernel(
    devices, sub, q_hbm, k_hbm, v_hbm, og_hbm, res_hbm, rate_hbm, gain_hbm,
    sum_ref, grad_ref, row_ref, q_ref, k_ref, v_ref, og_ref, state_ref, factor_ref, rise_ref,
    fall_ref, gain_ref, res_ref, rate_ref, stage, out_buf, in_buf, par_buf, par_all, state_buf, state_all,
    mixed_t, gated_t, conv_t, corr_t, second_buf, second_par, second_state,
    load_sems, out_send, out_recv, par_send, par_recv, state_send, state_recv,
    extra_send, extra_recv, ahead_send, ahead_recv, second_send,
):
    me = lax.axis_index("ctx") * sub + lax.axis_index("sub")
    channels, width = q_ref.shape
    blocks = width // LANES
    steps = width // GROUPS
    slab = 2 * blocks
    modes = res_ref.shape[1]
    f32, bf16 = jnp.float32, jnp.bfloat16
    peers = partners(me)
    place = place_of(me)
    far, near = among(place, FAR), among(place, [opposite(chip) for chip in FAR])
    across = index_of(*[lax.rem(v + 2, 4) for v in place[:3]], place[3])
    across_place = (across // sub, lax.rem(across, sub))
    barrier = pltpu.get_barrier_semaphore()
    for _, place in peers:
        pl.semaphore_signal(barrier, inc=1, device_id=place, device_id_type=MESH)
    loads = [
        pltpu.make_async_copy(src, dst, load_sems.at[i])
        for i, (src, dst) in enumerate(
            [(k_hbm, k_ref), (v_hbm, v_ref), (og_hbm, og_ref), (q_hbm, q_ref),
             (res_hbm, res_ref), (rate_hbm, rate_ref), (gain_hbm, gain_ref)]
        )
    ]
    for load in loads:
        load.start()
    for load in loads:
        load.wait()

    mixed_own = k_ref[...].astype(f32) * v_ref[...].astype(f32)
    gated_own = og_ref[...].astype(f32) * q_ref[...].astype(f32)
    for j in range(blocks):
        cols = slice(j * LANES, (j + 1) * LANES)
        stage[pl.ds(j, channels, stride=slab), :] = mixed_own[:, cols]
        stage[pl.ds(blocks + j, channels, stride=slab), :] = gated_own[:, cols]
    out_buf[...] = stage[...].astype(bf16).reshape(channels, slab, LANES)
    speed_row = jnp.exp(rate_ref[...])
    res_row = res_ref[...]
    par_buf[...] = jnp.zeros((1, LANES), f32)
    par_buf[:, 0:modes] = speed_row
    par_buf[:, modes : 2 * modes] = res_row

    pl.semaphore_wait(barrier, devices - 1)
    row_copy(par_buf, 0, second_par, 0, ahead_send, ahead_recv, across_place).start()
    send_all(peers, me, out_buf, in_buf, out_send, out_recv)
    for chip in FAR:
        for core in range(2):
            src, to = index_of(*chip, core), index_of(*opposite(chip), core)

            @pl.when(me != to)
            def _(src=src, to=to):
                row_copy(
                    out_buf, src, second_buf, me, extra_send, extra_recv, (to // sub, to % sub)
                ).start()

            @pl.when(me == to)
            def _(src=src, to=to):
                second_buf[to] = out_buf[src]

    send_all(peers, me, par_buf, par_all, par_send, par_recv)
    in_buf[me] = out_buf[me]
    par_all[pl.ds(me, 1), :] = par_buf[...]

    copies = LANES // modes
    half = copies // 2
    pos = iota((modes, width), 1).astype(f32)
    blank = jnp.zeros((half * modes, width), f32)

    def weights(speed):
        rise = jnp.exp(-speed * pos)
        fall = jnp.exp(-speed * (width - 1.0 - pos))
        to_end = jnp.concatenate([fall] * half + [blank], axis=0).astype(bf16)
        to_start = jnp.concatenate([blank] + [rise] * half, axis=0).astype(bf16)
        wide_speed = as_row(jnp.concatenate([speed] * copies, axis=0))
        return rise, fall, to_end, to_start, wide_speed

    speed = column(speed_row)
    rise, fall, to_end, to_start, wide_speed = weights(speed)
    to_end_timed = (fall * (width - 1.0 - pos)).astype(bf16)
    to_start_timed = (rise * pos).astype(bf16)
    grow = jnp.exp(speed * iota((modes, LANES), 1).astype(f32))
    mixed_own = (k_ref[...].astype(f32) * v_ref[...].astype(f32)).astype(bf16).astype(f32)
    gated_own = (og_ref[...].astype(f32) * q_ref[...].astype(f32)).astype(bf16).astype(f32)
    per_block = LANES // steps
    for own, turned in ((mixed_own, mixed_t), (gated_own, gated_t)):
        for j in range(blocks):
            block = own[:, j * LANES : (j + 1) * LANES].T
            for g in range(per_block):
                turned[pl.ds(j * per_block + g, steps, stride=GROUPS), :] = block[
                    g * steps : (g + 1) * steps, :
                ]

    row_copy(par_buf, 0, second_par, 0, ahead_send, ahead_recv, across_place).wait_recv()
    second_weights = weights(column(second_par[:, :modes]))[2:]

    def state(rows, weights):
        return lax.dot_general(rows, weights, NT, preferred_element_type=f32)

    def owned(buf, to_end, to_start, wide_speed):
        stage[...] = buf[...].reshape(devices * slab, LANES).astype(f32)

        def gathered(start):
            parts = [stage[pl.ds(start + j, devices, stride=slab), :] for j in range(blocks)]
            return jnp.concatenate(parts, axis=1).astype(bf16)

        mixed, gated = gathered(0), gathered(blocks)
        ends, starts = state(mixed, to_end), state(gated, to_start)
        before = running(ends, wide_speed, width, 1)
        after = running(starts, wide_speed, width, -1)
        return mixed, gated, starts, before, after

    whole(peers, in_buf, out_send, out_recv).wait_recv()
    mixed, gated, starts, before, after = owned(in_buf, to_end, to_start, wide_speed)

    @pl.when(jnp.logical_not(far))
    def _():
        state_buf[...] = before + after
        send_all(peers, me, state_buf, state_all, state_send, state_recv)
        state_all[pl.ds(me, 1), :] = state_buf[pl.ds(me, 1), :]

    @pl.when(near)
    def _():
        whole(peers, second_buf, extra_send, extra_recv).wait_recv()
        *_, before, after = owned(second_buf, *second_weights)
        second_state[...] = before + after
        send_all(peers, across, second_state, state_all, second_send, state_recv)
        state_all[pl.ds(across, 1), :] = second_state[pl.ds(me, 1), :]

    whole(peers, par_all, par_send, par_recv).wait_recv()
    params = par_all[...].T
    speeds = [jnp.broadcast_to(params[r : r + 1, :], (GROUPS, LANES)) for r in range(modes)]
    gains = [
        jnp.broadcast_to(params[modes + r : modes + r + 1, :], (GROUPS, LANES))
        for r in range(modes)
    ]
    decays = [jnp.exp(-x) for x in speeds]
    gain = column(gain_ref[...])
    for backward, own, x_ref, y_ref, to_ref in (
        (False, mixed_own, mixed_t, conv_t, sum_ref), (True, gated_own, gated_t, corr_t, grad_ref)
    ):
        found = scan_groups(x_ref, y_ref, steps, decays, gains, backward)
        sign = -1 if backward else 1
        inner = []
        for r in range(modes):
            sums = found[r]
            step = 1
            while step < GROUPS:
                sums = sums + jnp.exp(-speeds[r] * float(steps * step)) * shifted(sums, sign * step)
                step *= 2
            inner.append(gains[r] * shifted(sums, sign))
        add_states(y_ref, steps, decays, inner, backward)
        for j in range(blocks):
            cols = slice(j * LANES, (j + 1) * LANES)
            to_ref[:, cols] = natural(y_ref, steps, j) + gain * own[:, cols]

    lane = iota((channels, LANES), 1)
    own_gain = jnp.where((lane >= modes) & (lane < 2 * modes), par_all[...], 0.0)
    own_gain = pltpu.roll(own_gain, LANES - modes, 1)
    own_speed = jnp.where(lane < modes, par_all[...], 0.0)
    step = modes
    while step < LANES:
        own_gain = own_gain + pltpu.roll(own_gain, step, 1)
        own_speed = own_speed + pltpu.roll(own_speed, step, 1)
        step *= 2
    home = iota((channels, LANES), 0) % (2 * copies) - lane // modes
    for n in range(blocks):
        scaled = own_gain * jnp.exp(-own_speed * float(n * LANES))
        factor_ref[n, :, :LANES] = jnp.where(home == 0, scaled, 0.0)
        factor_ref[n, :, LANES:] = jnp.where(home == copies, scaled, 0.0)
    ahead = (iota((modes, LANES), 1) + 1).astype(f32)
    behind = (LANES - iota((modes, LANES), 1)).astype(f32)
    for c in range(channels):
        rate = -params[:modes, c : c + 1]
        rows = slice(c * modes, (c + 1) * modes)
        rise_ref[rows, :] = jnp.exp(rate * ahead).astype(bf16)
        fall_ref[rows, :] = jnp.exp(rate * behind).astype(bf16)

    pairs = lax.dot_general(mixed, gated, TN, preferred_element_type=f32)
    lag = iota((LANES, width), 1) - iota((LANES, width), 0)
    lagged = []
    for k in range(blocks):
        total = pairs[:LANES, k * LANES : (k + 1) * LANES]
        for row in range(1, blocks - k):
            rows = slice(row * LANES, (row + 1) * LANES)
            total = total + pairs[rows, (row + k) * LANES : (row + k + 1) * LANES]
        lagged.append(total)
    lagged = jnp.where(lag >= 0, jnp.concatenate(lagged, axis=1), 0.0)
    skip_sum = jnp.sum(jnp.where(lag == 0, lagged, 0.0), keepdims=True)

    def local_sum(values):
        by_lag = jnp.dot(grow, values, precision=FULL, preferred_element_type=f32)
        return jnp.sum(by_lag * rise, axis=1, keepdims=True)

    plain_col = local_sum(lagged)
    timed_col = local_sum(lagged * lag.astype(f32))
    one_step = jnp.exp(-speed_row)
    chunk_step = jnp.exp(-speed_row * float(width))
    ends_timed, starts_timed = state(mixed, to_end_timed), state(gated, to_start_timed)
    first, second = slice(0, modes), slice(half * modes, (half + 1) * modes)
    before, after, starts = before[:, first], after[:, second], starts[:, second]
    cross = before * starts
    cross_timed = ends_timed * after + before * starts_timed + cross
    cross_timed = cross_timed + (float(width) * chunk_step) * (before * after)
    plain = as_row(plain_col) + one_step * jnp.sum(cross, axis=0, keepdims=True)
    timed = as_row(timed_col) + one_step * jnp.sum(cross_timed, axis=0, keepdims=True)
    seq_len = devices * width
    row_ref[0:1, :] = jnp.zeros((1, LANES), f32)
    row_ref[0:1, 0:modes] = plain * (1.0 / seq_len)
    row_ref[0:1, modes : 2 * modes] = -res_row * speed_row * timed * (1.0 / seq_len**0.5)
    row_ref[0:1, 2 * modes : 2 * modes + 1] = skip_sum

    extras = 2 * len(FAR)
    whole(peers, in_buf, out_send, out_recv).wait_send()
    whole(peers, par_all, par_send, par_recv).wait_send()
    row_copy(par_buf, 0, second_par, 0, ahead_send, ahead_recv, across_place).wait_send()

    @pl.when(near)
    def _():
        whole(peers, second_buf, extra_send, extra_recv, extras - 1).wait_send()
        whole(peers, state_all, state_send, state_recv, devices - 2).wait_recv()
        whole(peers, state_all, second_send, state_recv).wait_send()

    @pl.when(jnp.logical_not(near))
    def _():
        whole(peers, second_buf, extra_send, extra_recv, extras).wait_send()

    @pl.when(far)
    def _():
        whole(peers, state_all, state_send, state_recv, devices).wait_recv()

    @pl.when(jnp.logical_not(jnp.logical_or(near, far)))
    def _():
        whole(peers, state_all, state_send, state_recv).wait_recv()

    @pl.when(jnp.logical_not(far))
    def _():
        whole(peers, state_all, state_send, state_recv).wait_send()

    state_ref[...] = state_all[...]


def finish_kernel(
    q_ref, k_ref, v_ref, og_ref, sum_ref, grad_ref, row_ref, state_ref, factor_ref, rise_ref,
    fall_ref, out_ref, gq_ref, gk_ref, gv_ref, gres_ref, grate_ref, gskip_ref,
):
    f32, bf16 = jnp.float32, jnp.bfloat16
    channels, width = q_ref.shape
    modes = gres_ref.shape[1]
    copies = LANES // modes
    gres_ref[...] = row_ref[:, 0:modes]
    grate_ref[...] = row_ref[:, modes : 2 * modes]
    gskip_ref[...] = row_ref[:, 2 * modes : 2 * modes + 1]
    blocks = width // LANES
    tall = 2 * copies
    states = state_ref[...]
    other = pltpu.roll(states, LANES // 2, 1)
    first = iota((channels, LANES), 1) < LANES // 2
    before = jnp.where(first, states, other)
    after = jnp.where(first, other, states)
    for g in range(channels // tall):
        rows = slice(g * tall, (g + 1) * tall)
        deep = slice(g * tall * modes, (g + 1) * tall * modes)
        for found, order, table_ref, base_ref, pair, places in (
            (before, 1, rise_ref, sum_ref, (q_ref, og_ref), (out_ref, gq_ref)),
            (after, -1, fall_ref, grad_ref, (v_ref, k_ref), (gk_ref, gv_ref)),
        ):
            own = jnp.concatenate([found[rows, :]] * 2, axis=1)
            parts = [own * factor_ref[n, rows, :] for n in range(blocks)][::order]
            share = jnp.dot(
                jnp.concatenate(parts, axis=0).astype(bf16),
                table_ref[deep, :],
                preferred_element_type=f32,
            )
            for n in range(blocks):
                cols = slice(n * LANES, (n + 1) * LANES)
                total = share[n * tall : (n + 1) * tall, :] + base_ref[rows, cols]
                for factor, place in zip(pair, places):
                    place[rows, cols] = (factor[rows, cols].astype(f32) * total).astype(bf16)


def body(queries, key_branch, value_branch, out_grad, residue, log_rate, skip_gain):
    sub = lax.axis_size("sub")
    devices = lax.axis_size("ctx") * sub
    channels, width = queries.shape
    modes = residue.shape[1]
    slab = 2 * width // LANES
    f32, bf16 = jnp.float32, jnp.bfloat16
    vmem = pl.BlockSpec(memory_space=pltpu.VMEM)
    wide = jax.ShapeDtypeStruct((channels, width), bf16)
    full = jax.ShapeDtypeStruct((channels, width), f32)
    square = jax.ShapeDtypeStruct((channels, LANES), f32)
    table = jax.ShapeDtypeStruct((channels * modes, LANES), bf16)
    factors = jax.ShapeDtypeStruct((width // LANES, channels, 2 * LANES), f32)
    hbm = pl.BlockSpec(memory_space=pltpu.HBM)
    operands = (queries, key_branch, value_branch, out_grad, residue, log_rate, skip_gain[None, :])
    total, grad, row, q, k, v, og, *states = pl.pallas_call(
        functools.partial(exchange_kernel, devices, sub),
        out_shape=(
            full, full, jax.ShapeDtypeStruct((1, LANES), f32), wide, wide, wide, wide,
            square, factors, table, table,
        ),
        in_specs=[hbm] * 7,
        out_specs=(vmem,) * 11,
        scratch_shapes=[
            pltpu.VMEM((1, channels), f32),
            pltpu.VMEM((1, modes), f32),
            pltpu.VMEM((1, modes), f32),
            pltpu.VMEM((channels * slab, LANES), f32),
            pltpu.VMEM((channels, slab, LANES), bf16),
            pltpu.VMEM((devices, slab, LANES), bf16),
            pltpu.VMEM((1, LANES), f32),
            pltpu.VMEM((channels, LANES), f32),
            pltpu.VMEM((devices, LANES), f32),
            pltpu.VMEM((channels, LANES), f32),
            pltpu.VMEM((width, LANES), f32),
            pltpu.VMEM((width, LANES), f32),
            pltpu.VMEM((width, LANES), f32),
            pltpu.VMEM((width, LANES), f32),
            pltpu.VMEM((devices, slab, LANES), bf16),
            pltpu.VMEM((1, LANES), f32),
            pltpu.VMEM((devices, LANES), f32),
            pltpu.SemaphoreType.DMA((7,)),
            pltpu.SemaphoreType.DMA,
            pltpu.SemaphoreType.DMA,
            pltpu.SemaphoreType.DMA,
            pltpu.SemaphoreType.DMA,
            pltpu.SemaphoreType.DMA,
            pltpu.SemaphoreType.DMA,
            pltpu.SemaphoreType.DMA,
            pltpu.SemaphoreType.DMA,
            pltpu.SemaphoreType.DMA,
            pltpu.SemaphoreType.DMA,
            pltpu.SemaphoreType.DMA,
        ],
        compiler_params=pltpu.CompilerParams(
            collective_id=0, has_side_effects=True, vmem_limit_bytes=32 * 2**20
        ),
        name="exchange",
    )(*[pltpu.with_memory_space_constraint(x, pltpu.HBM) for x in operands])
    output, grad_query, grad_key, grad_value, grad_residue, grad_rate, grad_skip = pl.pallas_call(
        finish_kernel,
        out_shape=(wide,) * 4
        + (jax.ShapeDtypeStruct((1, modes), f32),) * 2
        + (jax.ShapeDtypeStruct((1, 1), f32),),
        in_specs=[vmem] * 11,
        out_specs=(vmem,) * 7,
        compiler_params=pltpu.CompilerParams(vmem_limit_bytes=32 * 2**20),
        name="finish",
    )(q, k, v, og, total, grad, row, *states)
    return (
        output, grad_query, grad_key, grad_value, grad_residue, grad_rate, grad_skip.reshape(1)
    )


def solution(mesh):
    wide = P(None, ("ctx", "sub"))
    rows = P(("ctx", "sub"), None)
    return jax.shard_map(
        body,
        mesh=mesh,
        in_specs=(wide, wide, wide, wide, rows, rows, P()),
        out_specs=(wide, wide, wide, wide, rows, rows, P(("ctx", "sub"))),
        check_vma=False,
    )
```

```python
import functools
import random

import jax
import jax.numpy as jnp
from jax import lax
from jax.experimental import pallas as pl
from jax.experimental.pallas import tpu as pltpu
from jax.sharding import PartitionSpec as P

MESH = pl.DeviceIdType.MESH
FULL = lax.Precision.HIGHEST
NT = (((1,), (1,)), ((), ()))
TN = (((0,), (0,)), ((), ()))
LANES = 128
GROUPS = 8


MOVES = [
    (x, y, z, core)
    for x in range(4) for y in range(4) for z in range(4) for core in range(2)
    if (x, y, z, core) != (0, 0, 0, 0)
]


def far_first(weights, ties):
    def key(move):
        hops = [min(step, 4 - step) for step in move[:3]]
        return (-sum(w * h for w, h in zip(weights, hops)), ties(move))

    found = {move: key(move) for move in MOVES}
    return sorted(MOVES, key=lambda move: found[move])


MIXED = far_first((1, 1, 1), lambda m: (m[0] * 37 + m[1] * 11 + m[2] * 23 + m[3] * 5) % 16)
FIRST_ROUND = far_first((0.5, 1, 1.5), lambda m, draw=random.Random(0): draw.random())


def iota(shape, axis):
    return lax.broadcasted_iota(jnp.int32, shape, axis)


def column(row):
    n = row.shape[1]
    eye = iota((n, n), 0) == iota((n, n), 1)
    return jnp.sum(jnp.where(eye, row, 0.0), axis=1, keepdims=True)


def as_row(col):
    n = col.shape[0]
    eye = iota((n, n), 0) == iota((n, n), 1)
    return jnp.sum(jnp.where(eye, col, 0.0), axis=0, keepdims=True)


def shifted(rows, count):
    n = rows.shape[0]
    if count > 0:
        moved = pltpu.roll(rows, count, 0)
        return jnp.where(iota(rows.shape, 0) >= count, moved, 0.0)
    moved = pltpu.roll(rows, n + count, 0)
    return jnp.where(iota(rows.shape, 0) < n + count, moved, 0.0)


def running(rows, speed, span, sign):
    n = rows.shape[0]
    step = 1
    while step < n:
        rows = rows + jnp.exp(-speed * float(span * step)) * shifted(rows, sign * step)
        step *= 2
    return shifted(rows, sign)


def partners(me, moves):
    core, z = me % 2, me // 4 % 4
    y, x = me // 2 % 2 * 2 + me // 16 % 2, me // 32
    across = [lax.rem(x + d, 4) * 8 for d in range(4)]
    along = [lax.rem(z + d, 4) for d in range(4)]
    ups = [lax.rem(y + d, 4) for d in range(4)]
    high = [[u // 2 * 2 + lax.rem(core + d, 2) for d in range(2)] for u in ups]
    low = [lax.rem(u, 2) * 4 for u in ups]
    found = []
    for dx, dy, dz, dc in moves:
        ctx, sub = across[dx] + low[dy] + along[dz], high[dy][dc]
        found.append((ctx * 4 + sub, (ctx, sub)))
    return found


def send_all(peers, me, src, dst, send_sem, recv_sem):
    for peer, place in peers:
        row = 0 if src.shape[0] == 1 else peer
        pltpu.make_async_remote_copy(
            src_ref=src.at[pl.ds(row, 1)],
            dst_ref=dst.at[pl.ds(me, 1)],
            send_sem=send_sem,
            recv_sem=recv_sem,
            device_id=place,
            device_id_type=MESH,
        ).start()


def whole(peers, dst, send_sem, recv_sem):
    return pltpu.make_async_remote_copy(
        src_ref=dst.at[pl.ds(0, len(peers))],
        dst_ref=dst.at[pl.ds(0, len(peers))],
        send_sem=send_sem,
        recv_sem=recv_sem,
        device_id=peers[0][1],
        device_id_type=MESH,
    )


def loop_steps(count, unroll, step, carry):
    def some(i, carry):
        for j in range(unroll):
            carry = step(i * unroll + j, carry)
        return carry

    return lax.fori_loop(0, count // unroll, some, carry)


def tile_rows(step):
    return pl.ds(pl.multiple_of(step * GROUPS, GROUPS), GROUPS)


def scan_groups(x_ref, y_ref, steps, decays, gains, backward):
    def step(i, states):
        rows = tile_rows(steps - 1 - i if backward else i)
        x = x_ref[rows, :]
        states = [a * h + x for a, h in zip(decays, states)]
        y_ref[rows, :] = sum(g * h for g, h in zip(gains, states))
        return states

    start = [jnp.zeros((GROUPS, LANES), jnp.float32)] * len(decays)
    return loop_steps(steps, 4, step, start)


def add_states(y_ref, steps, decays, states, backward):
    def step(i, states):
        rows = tile_rows(steps - 1 - i if backward else i)
        states = [a * s for a, s in zip(decays, states)]
        y_ref[rows, :] = y_ref[rows, :] + sum(states)
        return states

    loop_steps(steps, 8, step, states)


def natural(y_ref, steps, j):
    per_block = LANES // steps
    parts = [
        y_ref[pl.ds(j * per_block + g, steps, stride=GROUPS), :] for g in range(per_block)
    ]
    return jnp.concatenate(parts, axis=0).T


def exchange_kernel(
    devices, sub, q_hbm, k_hbm, v_hbm, og_hbm, res_hbm, rate_hbm, gain_hbm,
    sum_ref, grad_ref, row_ref, q_ref, k_ref, v_ref, og_ref, state_ref, factor_ref, rise_ref,
    fall_ref, gain_ref, res_ref, rate_ref, stage, out_buf, in_buf, par_buf, par_all, state_buf, state_all,
    mixed_t, gated_t, conv_t, corr_t,
    load_sems, out_send, out_recv, par_send, par_recv, state_send, state_recv,
):
    me = lax.axis_index("ctx") * sub + lax.axis_index("sub")
    channels, width = q_ref.shape
    blocks = width // LANES
    steps = width // GROUPS
    slab = 2 * blocks
    modes = res_ref.shape[1]
    f32, bf16 = jnp.float32, jnp.bfloat16
    peers = partners(me, MIXED)
    barrier = pltpu.get_barrier_semaphore()
    for _, place in peers:
        pl.semaphore_signal(barrier, inc=1, device_id=place, device_id_type=MESH)
    loads = [
        pltpu.make_async_copy(src, dst, load_sems.at[i])
        for i, (src, dst) in enumerate(
            [(k_hbm, k_ref), (v_hbm, v_ref), (og_hbm, og_ref), (q_hbm, q_ref),
             (res_hbm, res_ref), (rate_hbm, rate_ref), (gain_hbm, gain_ref)]
        )
    ]
    for load in loads:
        load.start()
    for load in loads:
        load.wait()

    mixed_own = k_ref[...].astype(f32) * v_ref[...].astype(f32)
    gated_own = og_ref[...].astype(f32) * q_ref[...].astype(f32)
    for j in range(blocks):
        cols = slice(j * LANES, (j + 1) * LANES)
        stage[pl.ds(j, channels, stride=slab), :] = mixed_own[:, cols]
        stage[pl.ds(blocks + j, channels, stride=slab), :] = gated_own[:, cols]
    out_buf[...] = stage[...].astype(bf16).reshape(channels, slab, LANES)
    speed_row = jnp.exp(rate_ref[...])
    res_row = res_ref[...]
    par_buf[...] = jnp.zeros((1, LANES), f32)
    par_buf[:, 0:modes] = speed_row
    par_buf[:, modes : 2 * modes] = res_row

    pl.semaphore_wait(barrier, devices - 1)
    send_all(partners(me, FIRST_ROUND), me, out_buf, in_buf, out_send, out_recv)
    send_all(peers, me, par_buf, par_all, par_send, par_recv)
    in_buf[me] = out_buf[me]
    par_all[pl.ds(me, 1), :] = par_buf[...]

    speed = column(speed_row)
    copies = LANES // modes
    half = copies // 2
    wide_speed = as_row(jnp.concatenate([speed] * copies, axis=0))
    pos = iota((modes, width), 1).astype(f32)
    rise = jnp.exp(-speed * pos)
    fall = jnp.exp(-speed * (width - 1.0 - pos))
    blank = jnp.zeros((half * modes, width), f32)
    to_end = jnp.concatenate([fall] * half + [blank], axis=0).astype(bf16)
    to_start = jnp.concatenate([blank] + [rise] * half, axis=0).astype(bf16)
    to_end_timed = (fall * (width - 1.0 - pos)).astype(bf16)
    to_start_timed = (rise * pos).astype(bf16)
    grow = jnp.exp(speed * iota((modes, LANES), 1).astype(f32))
    mixed_own = (k_ref[...].astype(f32) * v_ref[...].astype(f32)).astype(bf16).astype(f32)
    gated_own = (og_ref[...].astype(f32) * q_ref[...].astype(f32)).astype(bf16).astype(f32)
    per_block = LANES // steps
    for own, turned in ((mixed_own, mixed_t), (gated_own, gated_t)):
        for j in range(blocks):
            block = own[:, j * LANES : (j + 1) * LANES].T
            for g in range(per_block):
                turned[pl.ds(j * per_block + g, steps, stride=GROUPS), :] = block[
                    g * steps : (g + 1) * steps, :
                ]

    whole(peers, in_buf, out_send, out_recv).wait_recv()
    stage[...] = in_buf[...].reshape(devices * slab, LANES).astype(f32)

    def gathered(start):
        parts = [stage[pl.ds(start + j, devices, stride=slab), :] for j in range(blocks)]
        return jnp.concatenate(parts, axis=1).astype(bf16)

    mixed, gated = gathered(0), gathered(blocks)

    def state(rows, weights):
        return lax.dot_general(rows, weights, NT, preferred_element_type=f32)

    ends, starts = state(mixed, to_end), state(gated, to_start)
    before = running(ends, wide_speed, width, 1)
    after = running(starts, wide_speed, width, -1)
    state_buf[...] = before + after
    send_all(peers, me, state_buf, state_all, state_send, state_recv)
    state_all[pl.ds(me, 1), :] = state_buf[pl.ds(me, 1), :]

    whole(peers, par_all, par_send, par_recv).wait_recv()
    params = par_all[...].T
    speeds = [jnp.broadcast_to(params[r : r + 1, :], (GROUPS, LANES)) for r in range(modes)]
    gains = [
        jnp.broadcast_to(params[modes + r : modes + r + 1, :], (GROUPS, LANES))
        for r in range(modes)
    ]
    decays = [jnp.exp(-x) for x in speeds]
    gain = column(gain_ref[...])
    for backward, own, x_ref, y_ref, to_ref in (
        (False, mixed_own, mixed_t, conv_t, sum_ref), (True, gated_own, gated_t, corr_t, grad_ref)
    ):
        found = scan_groups(x_ref, y_ref, steps, decays, gains, backward)
        sign = -1 if backward else 1
        inner = []
        for r in range(modes):
            sums = found[r]
            step = 1
            while step < GROUPS:
                sums = sums + jnp.exp(-speeds[r] * float(steps * step)) * shifted(sums, sign * step)
                step *= 2
            inner.append(gains[r] * shifted(sums, sign))
        add_states(y_ref, steps, decays, inner, backward)
        for j in range(blocks):
            cols = slice(j * LANES, (j + 1) * LANES)
            to_ref[:, cols] = natural(y_ref, steps, j) + gain * own[:, cols]

    lane = iota((channels, LANES), 1)
    own_gain = jnp.where((lane >= modes) & (lane < 2 * modes), par_all[...], 0.0)
    own_gain = pltpu.roll(own_gain, LANES - modes, 1)
    own_speed = jnp.where(lane < modes, par_all[...], 0.0)
    step = modes
    while step < LANES:
        own_gain = own_gain + pltpu.roll(own_gain, step, 1)
        own_speed = own_speed + pltpu.roll(own_speed, step, 1)
        step *= 2
    home = iota((channels, LANES), 0) % (2 * copies) - lane // modes
    for n in range(blocks):
        scaled = own_gain * jnp.exp(-own_speed * float(n * LANES))
        factor_ref[n, :, :LANES] = jnp.where(home == 0, scaled, 0.0)
        factor_ref[n, :, LANES:] = jnp.where(home == copies, scaled, 0.0)
    ahead = (iota((modes, LANES), 1) + 1).astype(f32)
    behind = (LANES - iota((modes, LANES), 1)).astype(f32)
    for c in range(channels):
        rate = -params[:modes, c : c + 1]
        rows = slice(c * modes, (c + 1) * modes)
        rise_ref[rows, :] = jnp.exp(rate * ahead).astype(bf16)
        fall_ref[rows, :] = jnp.exp(rate * behind).astype(bf16)

    pairs = lax.dot_general(mixed, gated, TN, preferred_element_type=f32)
    lag = iota((LANES, width), 1) - iota((LANES, width), 0)
    lagged = []
    for k in range(blocks):
        total = pairs[:LANES, k * LANES : (k + 1) * LANES]
        for row in range(1, blocks - k):
            rows = slice(row * LANES, (row + 1) * LANES)
            total = total + pairs[rows, (row + k) * LANES : (row + k + 1) * LANES]
        lagged.append(total)
    lagged = jnp.where(lag >= 0, jnp.concatenate(lagged, axis=1), 0.0)
    skip_sum = jnp.sum(jnp.where(lag == 0, lagged, 0.0), keepdims=True)

    def local_sum(values):
        by_lag = jnp.dot(grow, values, precision=FULL, preferred_element_type=f32)
        return jnp.sum(by_lag * rise, axis=1, keepdims=True)

    plain_col = local_sum(lagged)
    timed_col = local_sum(lagged * lag.astype(f32))
    one_step = jnp.exp(-speed_row)
    chunk_step = jnp.exp(-speed_row * float(width))
    ends_timed, starts_timed = state(mixed, to_end_timed), state(gated, to_start_timed)
    first, second = slice(0, modes), slice(half * modes, (half + 1) * modes)
    before, after, starts = before[:, first], after[:, second], starts[:, second]
    cross = before * starts
    cross_timed = ends_timed * after + before * starts_timed + cross
    cross_timed = cross_timed + (float(width) * chunk_step) * (before * after)
    plain = as_row(plain_col) + one_step * jnp.sum(cross, axis=0, keepdims=True)
    timed = as_row(timed_col) + one_step * jnp.sum(cross_timed, axis=0, keepdims=True)
    seq_len = devices * width
    row_ref[0:1, :] = jnp.zeros((1, LANES), f32)
    row_ref[0:1, 0:modes] = plain * (1.0 / seq_len)
    row_ref[0:1, modes : 2 * modes] = -res_row * speed_row * timed * (1.0 / seq_len**0.5)
    row_ref[0:1, 2 * modes : 2 * modes + 1] = skip_sum

    whole(peers, in_buf, out_send, out_recv).wait_send()
    whole(peers, par_all, par_send, par_recv).wait_send()
    whole(peers, state_all, state_send, state_recv).wait_recv()
    state_ref[...] = state_all[...]
    whole(peers, state_all, state_send, state_recv).wait_send()


def finish_kernel(
    q_ref, k_ref, v_ref, og_ref, sum_ref, grad_ref, row_ref, state_ref, factor_ref, rise_ref,
    fall_ref, out_ref, gq_ref, gk_ref, gv_ref, gres_ref, grate_ref, gskip_ref,
):
    f32, bf16 = jnp.float32, jnp.bfloat16
    channels, width = q_ref.shape
    modes = gres_ref.shape[1]
    copies = LANES // modes
    gres_ref[...] = row_ref[:, 0:modes]
    grate_ref[...] = row_ref[:, modes : 2 * modes]
    gskip_ref[...] = row_ref[:, 2 * modes : 2 * modes + 1]
    blocks = width // LANES
    tall = 2 * copies
    states = state_ref[...]
    other = pltpu.roll(states, LANES // 2, 1)
    first = iota((channels, LANES), 1) < LANES // 2
    before = jnp.where(first, states, other)
    after = jnp.where(first, other, states)
    for g in range(channels // tall):
        rows = slice(g * tall, (g + 1) * tall)
        deep = slice(g * tall * modes, (g + 1) * tall * modes)
        for found, order, table_ref, base_ref, pair, places in (
            (before, 1, rise_ref, sum_ref, (q_ref, og_ref), (out_ref, gq_ref)),
            (after, -1, fall_ref, grad_ref, (v_ref, k_ref), (gk_ref, gv_ref)),
        ):
            own = jnp.concatenate([found[rows, :]] * 2, axis=1)
            parts = [own * factor_ref[n, rows, :] for n in range(blocks)][::order]
            share = jnp.dot(
                jnp.concatenate(parts, axis=0).astype(bf16),
                table_ref[deep, :],
                preferred_element_type=f32,
            )
            for n in range(blocks):
                cols = slice(n * LANES, (n + 1) * LANES)
                total = share[n * tall : (n + 1) * tall, :] + base_ref[rows, cols]
                for factor, place in zip(pair, places):
                    place[rows, cols] = (factor[rows, cols].astype(f32) * total).astype(bf16)


def body(queries, key_branch, value_branch, out_grad, residue, log_rate, skip_gain):
    sub = lax.axis_size("sub")
    devices = lax.axis_size("ctx") * sub
    channels, width = queries.shape
    modes = residue.shape[1]
    slab = 2 * width // LANES
    f32, bf16 = jnp.float32, jnp.bfloat16
    vmem = pl.BlockSpec(memory_space=pltpu.VMEM)
    wide = jax.ShapeDtypeStruct((channels, width), bf16)
    full = jax.ShapeDtypeStruct((channels, width), f32)
    square = jax.ShapeDtypeStruct((channels, LANES), f32)
    table = jax.ShapeDtypeStruct((channels * modes, LANES), bf16)
    factors = jax.ShapeDtypeStruct((width // LANES, channels, 2 * LANES), f32)
    hbm = pl.BlockSpec(memory_space=pltpu.HBM)
    operands = (queries, key_branch, value_branch, out_grad, residue, log_rate, skip_gain[None, :])
    total, grad, row, q, k, v, og, *states = pl.pallas_call(
        functools.partial(exchange_kernel, devices, sub),
        out_shape=(
            full, full, jax.ShapeDtypeStruct((1, LANES), f32), wide, wide, wide, wide,
            square, factors, table, table,
        ),
        in_specs=[hbm] * 7,
        out_specs=(vmem,) * 11,
        scratch_shapes=[
            pltpu.VMEM((1, channels), f32),
            pltpu.VMEM((1, modes), f32),
            pltpu.VMEM((1, modes), f32),
            pltpu.VMEM((channels * slab, LANES), f32),
            pltpu.VMEM((channels, slab, LANES), bf16),
            pltpu.VMEM((devices, slab, LANES), bf16),
            pltpu.VMEM((1, LANES), f32),
            pltpu.VMEM((channels, LANES), f32),
            pltpu.VMEM((devices, LANES), f32),
            pltpu.VMEM((channels, LANES), f32),
            pltpu.VMEM((width, LANES), f32),
            pltpu.VMEM((width, LANES), f32),
            pltpu.VMEM((width, LANES), f32),
            pltpu.VMEM((width, LANES), f32),
            pltpu.SemaphoreType.DMA((7,)),
            pltpu.SemaphoreType.DMA,
            pltpu.SemaphoreType.DMA,
            pltpu.SemaphoreType.DMA,
            pltpu.SemaphoreType.DMA,
            pltpu.SemaphoreType.DMA,
            pltpu.SemaphoreType.DMA,
        ],
        compiler_params=pltpu.CompilerParams(
            collective_id=0, has_side_effects=True, vmem_limit_bytes=32 * 2**20
        ),
        name="exchange",
    )(*[pltpu.with_memory_space_constraint(x, pltpu.HBM) for x in operands])
    output, grad_query, grad_key, grad_value, grad_residue, grad_rate, grad_skip = pl.pallas_call(
        finish_kernel,
        out_shape=(wide,) * 4
        + (jax.ShapeDtypeStruct((1, modes), f32),) * 2
        + (jax.ShapeDtypeStruct((1, 1), f32),),
        in_specs=[vmem] * 11,
        out_specs=(vmem,) * 7,
        compiler_params=pltpu.CompilerParams(vmem_limit_bytes=32 * 2**20),
        name="finish",
    )(q, k, v, og, total, grad, row, *states)
    return (
        output, grad_query, grad_key, grad_value, grad_residue, grad_rate, grad_skip.reshape(1)
    )


def solution(mesh):
    wide = P(None, ("ctx", "sub"))
    rows = P(("ctx", "sub"), None)
    return jax.shard_map(
        body,
        mesh=mesh,
        in_specs=(wide, wide, wide, wide, rows, rows, P()),
        out_specs=(wide, wide, wide, wide, rows, rows, P(("ctx", "sub"))),
        check_vma=False,
    )
```

```python
import functools
import random

import jax
import jax.numpy as jnp
from jax import lax
from jax.experimental import pallas as pl
from jax.experimental.pallas import tpu as pltpu
from jax.sharding import PartitionSpec as P

MESH = pl.DeviceIdType.MESH
FULL = lax.Precision.HIGHEST
NT = (((1,), (1,)), ((), ()))
TN = (((0,), (0,)), ((), ()))
LANES = 128
GROUPS = 8


MOVES = [
    (x, y, z, core)
    for x in range(4) for y in range(4) for z in range(4) for core in range(2)
    if (x, y, z, core) != (0, 0, 0, 0)
]


def far_first(weights, ties):
    def key(move):
        hops = [min(step, 4 - step) for step in move[:3]]
        return (-sum(w * h for w, h in zip(weights, hops)), ties(move))

    found = {move: key(move) for move in MOVES}
    return sorted(MOVES, key=lambda move: found[move])


MIXED = far_first((1, 1, 1), lambda m: (m[0] * 37 + m[1] * 11 + m[2] * 23 + m[3] * 5) % 16)
FIRST_ROUND = far_first((0.5, 1, 1.5), lambda m, draw=random.Random(0): draw.random())
LAST_ROUND = far_first((1, 1, 1), lambda m, draw=random.Random(0): draw.random())


def iota(shape, axis):
    return lax.broadcasted_iota(jnp.int32, shape, axis)


def column(row):
    n = row.shape[1]
    eye = iota((n, n), 0) == iota((n, n), 1)
    return jnp.sum(jnp.where(eye, row, 0.0), axis=1, keepdims=True)


def as_row(col):
    n = col.shape[0]
    eye = iota((n, n), 0) == iota((n, n), 1)
    return jnp.sum(jnp.where(eye, col, 0.0), axis=0, keepdims=True)


def shifted(rows, count):
    n = rows.shape[0]
    if count > 0:
        moved = pltpu.roll(rows, count, 0)
        return jnp.where(iota(rows.shape, 0) >= count, moved, 0.0)
    moved = pltpu.roll(rows, n + count, 0)
    return jnp.where(iota(rows.shape, 0) < n + count, moved, 0.0)


def running(rows, speed, span, sign):
    n = rows.shape[0]
    step = 1
    while step < n:
        rows = rows + jnp.exp(-speed * float(span * step)) * shifted(rows, sign * step)
        step *= 2
    return shifted(rows, sign)


def partners(me, moves):
    core, z = me % 2, me // 4 % 4
    y, x = me // 2 % 2 * 2 + me // 16 % 2, me // 32
    across = [lax.rem(x + d, 4) * 8 for d in range(4)]
    along = [lax.rem(z + d, 4) for d in range(4)]
    ups = [lax.rem(y + d, 4) for d in range(4)]
    high = [[u // 2 * 2 + lax.rem(core + d, 2) for d in range(2)] for u in ups]
    low = [lax.rem(u, 2) * 4 for u in ups]
    found = []
    for dx, dy, dz, dc in moves:
        ctx, sub = across[dx] + low[dy] + along[dz], high[dy][dc]
        found.append((ctx * 4 + sub, (ctx, sub)))
    return found


def send_all(peers, me, src, dst, send_sem, recv_sem):
    for peer, place in peers:
        row = 0 if src.shape[0] == 1 else peer
        pltpu.make_async_remote_copy(
            src_ref=src.at[pl.ds(row, 1)],
            dst_ref=dst.at[pl.ds(me, 1)],
            send_sem=send_sem,
            recv_sem=recv_sem,
            device_id=place,
            device_id_type=MESH,
        ).start()


def whole(peers, dst, send_sem, recv_sem):
    return pltpu.make_async_remote_copy(
        src_ref=dst.at[pl.ds(0, len(peers))],
        dst_ref=dst.at[pl.ds(0, len(peers))],
        send_sem=send_sem,
        recv_sem=recv_sem,
        device_id=peers[0][1],
        device_id_type=MESH,
    )


def loop_steps(count, unroll, step, carry):
    def some(i, carry):
        for j in range(unroll):
            carry = step(i * unroll + j, carry)
        return carry

    return lax.fori_loop(0, count // unroll, some, carry)


def tile_rows(step):
    return pl.ds(pl.multiple_of(step * GROUPS, GROUPS), GROUPS)


def scan_groups(x_ref, y_ref, steps, decays, gains, backward):
    def step(i, states):
        rows = tile_rows(steps - 1 - i if backward else i)
        x = x_ref[rows, :]
        states = [a * h + x for a, h in zip(decays, states)]
        y_ref[rows, :] = sum(g * h for g, h in zip(gains, states))
        return states

    start = [jnp.zeros((GROUPS, LANES), jnp.float32)] * len(decays)
    return loop_steps(steps, 4, step, start)


def add_states(y_ref, steps, decays, states, backward):
    def step(i, states):
        rows = tile_rows(steps - 1 - i if backward else i)
        states = [a * s for a, s in zip(decays, states)]
        y_ref[rows, :] = y_ref[rows, :] + sum(states)
        return states

    loop_steps(steps, 8, step, states)


def natural(y_ref, steps, j):
    per_block = LANES // steps
    parts = [
        y_ref[pl.ds(j * per_block + g, steps, stride=GROUPS), :] for g in range(per_block)
    ]
    return jnp.concatenate(parts, axis=0).T


def exchange_kernel(
    devices, sub, q_hbm, k_hbm, v_hbm, og_hbm, res_hbm, rate_hbm, gain_hbm,
    sum_ref, grad_ref, row_ref, q_ref, k_ref, v_ref, og_ref, state_ref, factor_ref, rise_ref,
    fall_ref, gain_ref, res_ref, rate_ref, stage, out_buf, in_buf, par_buf, par_all, state_buf, state_all,
    mixed_t, gated_t, conv_t, corr_t,
    load_sems, out_send, out_recv, par_send, par_recv, state_send, state_recv,
):
    me = lax.axis_index("ctx") * sub + lax.axis_index("sub")
    channels, width = q_ref.shape
    blocks = width // LANES
    steps = width // GROUPS
    slab = 2 * blocks
    modes = res_ref.shape[1]
    f32, bf16 = jnp.float32, jnp.bfloat16
    peers = partners(me, MIXED)
    barrier = pltpu.get_barrier_semaphore()
    for _, place in peers:
        pl.semaphore_signal(barrier, inc=1, device_id=place, device_id_type=MESH)
    loads = [
        pltpu.make_async_copy(src, dst, load_sems.at[i])
        for i, (src, dst) in enumerate(
            [(k_hbm, k_ref), (v_hbm, v_ref), (og_hbm, og_ref), (q_hbm, q_ref),
             (res_hbm, res_ref), (rate_hbm, rate_ref), (gain_hbm, gain_ref)]
        )
    ]
    for load in loads:
        load.start()
    for load in loads:
        load.wait()

    mixed_own = k_ref[...].astype(f32) * v_ref[...].astype(f32)
    gated_own = og_ref[...].astype(f32) * q_ref[...].astype(f32)
    for j in range(blocks):
        cols = slice(j * LANES, (j + 1) * LANES)
        stage[pl.ds(j, channels, stride=slab), :] = mixed_own[:, cols]
        stage[pl.ds(blocks + j, channels, stride=slab), :] = gated_own[:, cols]
    out_buf[...] = stage[...].astype(bf16).reshape(channels, slab, LANES)
    speed_row = jnp.exp(rate_ref[...])
    res_row = res_ref[...]
    par_buf[...] = jnp.zeros((1, LANES), f32)
    par_buf[:, 0:modes] = speed_row
    par_buf[:, modes : 2 * modes] = res_row

    pl.semaphore_wait(barrier, devices - 1)
    send_all(partners(me, FIRST_ROUND), me, out_buf, in_buf, out_send, out_recv)
    send_all(peers, me, par_buf, par_all, par_send, par_recv)
    in_buf[me] = out_buf[me]
    par_all[pl.ds(me, 1), :] = par_buf[...]

    speed = column(speed_row)
    copies = LANES // modes
    half = copies // 2
    wide_speed = as_row(jnp.concatenate([speed] * copies, axis=0))
    pos = iota((modes, width), 1).astype(f32)
    rise = jnp.exp(-speed * pos)
    fall = jnp.exp(-speed * (width - 1.0 - pos))
    blank = jnp.zeros((half * modes, width), f32)
    to_end = jnp.concatenate([fall] * half + [blank], axis=0).astype(bf16)
    to_start = jnp.concatenate([blank] + [rise] * half, axis=0).astype(bf16)
    to_end_timed = (fall * (width - 1.0 - pos)).astype(bf16)
    to_start_timed = (rise * pos).astype(bf16)
    grow = jnp.exp(speed * iota((modes, LANES), 1).astype(f32))
    mixed_own = (k_ref[...].astype(f32) * v_ref[...].astype(f32)).astype(bf16).astype(f32)
    gated_own = (og_ref[...].astype(f32) * q_ref[...].astype(f32)).astype(bf16).astype(f32)
    per_block = LANES // steps
    for own, turned in ((mixed_own, mixed_t), (gated_own, gated_t)):
        for j in range(blocks):
            block = own[:, j * LANES : (j + 1) * LANES].T
            for g in range(per_block):
                turned[pl.ds(j * per_block + g, steps, stride=GROUPS), :] = block[
                    g * steps : (g + 1) * steps, :
                ]

    whole(peers, in_buf, out_send, out_recv).wait_recv()
    stage[...] = in_buf[...].reshape(devices * slab, LANES).astype(f32)

    def gathered(start):
        parts = [stage[pl.ds(start + j, devices, stride=slab), :] for j in range(blocks)]
        return jnp.concatenate(parts, axis=1).astype(bf16)

    mixed, gated = gathered(0), gathered(blocks)

    def state(rows, weights):
        return lax.dot_general(rows, weights, NT, preferred_element_type=f32)

    ends, starts = state(mixed, to_end), state(gated, to_start)
    before = running(ends, wide_speed, width, 1)
    after = running(starts, wide_speed, width, -1)
    state_buf[...] = before + after
    send_all(partners(me, LAST_ROUND), me, state_buf, state_all, state_send, state_recv)
    state_all[pl.ds(me, 1), :] = state_buf[pl.ds(me, 1), :]

    whole(peers, par_all, par_send, par_recv).wait_recv()
    params = par_all[...].T
    speeds = [jnp.broadcast_to(params[r : r + 1, :], (GROUPS, LANES)) for r in range(modes)]
    gains = [
        jnp.broadcast_to(params[modes + r : modes + r + 1, :], (GROUPS, LANES))
        for r in range(modes)
    ]
    decays = [jnp.exp(-x) for x in speeds]
    gain = column(gain_ref[...])
    for backward, own, x_ref, y_ref, to_ref in (
        (False, mixed_own, mixed_t, conv_t, sum_ref), (True, gated_own, gated_t, corr_t, grad_ref)
    ):
        found = scan_groups(x_ref, y_ref, steps, decays, gains, backward)
        sign = -1 if backward else 1
        inner = []
        for r in range(modes):
            sums = found[r]
            step = 1
            while step < GROUPS:
                sums = sums + jnp.exp(-speeds[r] * float(steps * step)) * shifted(sums, sign * step)
                step *= 2
            inner.append(gains[r] * shifted(sums, sign))
        add_states(y_ref, steps, decays, inner, backward)
        for j in range(blocks):
            cols = slice(j * LANES, (j + 1) * LANES)
            to_ref[:, cols] = natural(y_ref, steps, j) + gain * own[:, cols]

    lane = iota((channels, LANES), 1)
    own_gain = jnp.where((lane >= modes) & (lane < 2 * modes), par_all[...], 0.0)
    own_gain = pltpu.roll(own_gain, LANES - modes, 1)
    own_speed = jnp.where(lane < modes, par_all[...], 0.0)
    step = modes
    while step < LANES:
        own_gain = own_gain + pltpu.roll(own_gain, step, 1)
        own_speed = own_speed + pltpu.roll(own_speed, step, 1)
        step *= 2
    home = iota((channels, LANES), 0) % (2 * copies) - lane // modes
    for n in range(blocks):
        scaled = own_gain * jnp.exp(-own_speed * float(n * LANES))
        factor_ref[n, :, :LANES] = jnp.where(home == 0, scaled, 0.0).astype(bf16)
        factor_ref[n, :, LANES:] = jnp.where(home == copies, scaled, 0.0).astype(bf16)
    ahead = (iota((modes, LANES), 1) + 1).astype(f32)
    behind = (LANES - iota((modes, LANES), 1)).astype(f32)
    for c in range(channels):
        rate = -params[:modes, c : c + 1]
        rows = slice(c * modes, (c + 1) * modes)
        rise_ref[rows, :] = jnp.exp(rate * ahead).astype(bf16)
        fall_ref[rows, :] = jnp.exp(rate * behind).astype(bf16)

    pairs = lax.dot_general(mixed, gated, TN, preferred_element_type=f32)
    lag = iota((LANES, width), 1) - iota((LANES, width), 0)
    lagged = []
    for k in range(blocks):
        total = pairs[:LANES, k * LANES : (k + 1) * LANES]
        for row in range(1, blocks - k):
            rows = slice(row * LANES, (row + 1) * LANES)
            total = total + pairs[rows, (row + k) * LANES : (row + k + 1) * LANES]
        lagged.append(total)
    lagged = jnp.where(lag >= 0, jnp.concatenate(lagged, axis=1), 0.0)
    skip_sum = jnp.sum(jnp.where(lag == 0, lagged, 0.0), keepdims=True)

    def local_sum(values):
        by_lag = jnp.dot(grow, values, precision=FULL, preferred_element_type=f32)
        return jnp.sum(by_lag * rise, axis=1, keepdims=True)

    plain_col = local_sum(lagged)
    timed_col = local_sum(lagged * lag.astype(f32))
    one_step = jnp.exp(-speed_row)
    chunk_step = jnp.exp(-speed_row * float(width))
    ends_timed, starts_timed = state(mixed, to_end_timed), state(gated, to_start_timed)
    first, second = slice(0, modes), slice(half * modes, (half + 1) * modes)
    before, after, starts = before[:, first], after[:, second], starts[:, second]
    cross = before * starts
    cross_timed = ends_timed * after + before * starts_timed + cross
    cross_timed = cross_timed + (float(width) * chunk_step) * (before * after)
    plain = as_row(plain_col) + one_step * jnp.sum(cross, axis=0, keepdims=True)
    timed = as_row(timed_col) + one_step * jnp.sum(cross_timed, axis=0, keepdims=True)
    seq_len = devices * width
    row_ref[0:1, :] = jnp.zeros((1, LANES), f32)
    row_ref[0:1, 0:modes] = plain * (1.0 / seq_len)
    row_ref[0:1, modes : 2 * modes] = -res_row * speed_row * timed * (1.0 / seq_len**0.5)
    row_ref[0:1, 2 * modes : 2 * modes + 1] = skip_sum

    whole(peers, in_buf, out_send, out_recv).wait_send()
    whole(peers, par_all, par_send, par_recv).wait_send()
    whole(peers, state_all, state_send, state_recv).wait_recv()
    state_ref[...] = state_all[...]
    whole(peers, state_all, state_send, state_recv).wait_send()


def finish_kernel(
    q_ref, k_ref, v_ref, og_ref, sum_ref, grad_ref, row_ref, state_ref, factor_ref, rise_ref,
    fall_ref, out_ref, gq_ref, gk_ref, gv_ref, gres_ref, grate_ref, gskip_ref,
):
    f32, bf16 = jnp.float32, jnp.bfloat16
    channels, width = q_ref.shape
    modes = gres_ref.shape[1]
    copies = LANES // modes
    gres_ref[...] = row_ref[:, 0:modes]
    grate_ref[...] = row_ref[:, modes : 2 * modes]
    gskip_ref[...] = row_ref[:, 2 * modes : 2 * modes + 1]
    blocks = width // LANES
    tall = 2 * copies
    states = state_ref[...]
    other = pltpu.roll(states, LANES // 2, 1)
    first = iota((channels, LANES), 1) < LANES // 2
    before = jnp.where(first, states, other).astype(bf16)
    after = jnp.where(first, other, states).astype(bf16)
    for g in range(channels // tall):
        rows = slice(g * tall, (g + 1) * tall)
        deep = slice(g * tall * modes, (g + 1) * tall * modes)
        for found, order, table_ref, base_ref, pair, places in (
            (before, 1, rise_ref, sum_ref, (q_ref, og_ref), (out_ref, gq_ref)),
            (after, -1, fall_ref, grad_ref, (v_ref, k_ref), (gk_ref, gv_ref)),
        ):
            own = jnp.concatenate([found[rows, :]] * 2, axis=1)
            parts = [own * factor_ref[n, rows, :] for n in range(blocks)][::order]
            share = jnp.dot(
                jnp.concatenate(parts, axis=0),
                table_ref[deep, :],
                preferred_element_type=f32,
            )
            for n in range(blocks):
                cols = slice(n * LANES, (n + 1) * LANES)
                total = share[n * tall : (n + 1) * tall, :] + base_ref[rows, cols]
                for factor, place in zip(pair, places):
                    place[rows, cols] = (factor[rows, cols].astype(f32) * total).astype(bf16)


def body(queries, key_branch, value_branch, out_grad, residue, log_rate, skip_gain):
    sub = lax.axis_size("sub")
    devices = lax.axis_size("ctx") * sub
    channels, width = queries.shape
    modes = residue.shape[1]
    slab = 2 * width // LANES
    f32, bf16 = jnp.float32, jnp.bfloat16
    vmem = pl.BlockSpec(memory_space=pltpu.VMEM)
    wide = jax.ShapeDtypeStruct((channels, width), bf16)
    full = jax.ShapeDtypeStruct((channels, width), f32)
    square = jax.ShapeDtypeStruct((channels, LANES), f32)
    table = jax.ShapeDtypeStruct((channels * modes, LANES), bf16)
    factors = jax.ShapeDtypeStruct((width // LANES, channels, 2 * LANES), bf16)
    hbm = pl.BlockSpec(memory_space=pltpu.HBM)
    operands = (queries, key_branch, value_branch, out_grad, residue, log_rate, skip_gain[None, :])
    total, grad, row, q, k, v, og, *states = pl.pallas_call(
        functools.partial(exchange_kernel, devices, sub),
        out_shape=(
            full, full, jax.ShapeDtypeStruct((1, LANES), f32), wide, wide, wide, wide,
            square, factors, table, table,
        ),
        in_specs=[hbm] * 7,
        out_specs=(vmem,) * 11,
        scratch_shapes=[
            pltpu.VMEM((1, channels), f32),
            pltpu.VMEM((1, modes), f32),
            pltpu.VMEM((1, modes), f32),
            pltpu.VMEM((channels * slab, LANES), f32),
            pltpu.VMEM((channels, slab, LANES), bf16),
            pltpu.VMEM((devices, slab, LANES), bf16),
            pltpu.VMEM((1, LANES), f32),
            pltpu.VMEM((channels, LANES), f32),
            pltpu.VMEM((devices, LANES), f32),
            pltpu.VMEM((channels, LANES), f32),
            pltpu.VMEM((width, LANES), f32),
            pltpu.VMEM((width, LANES), f32),
            pltpu.VMEM((width, LANES), f32),
            pltpu.VMEM((width, LANES), f32),
            pltpu.SemaphoreType.DMA((7,)),
            pltpu.SemaphoreType.DMA,
            pltpu.SemaphoreType.DMA,
            pltpu.SemaphoreType.DMA,
            pltpu.SemaphoreType.DMA,
            pltpu.SemaphoreType.DMA,
            pltpu.SemaphoreType.DMA,
        ],
        compiler_params=pltpu.CompilerParams(
            collective_id=0, has_side_effects=True, vmem_limit_bytes=32 * 2**20
        ),
        name="exchange",
    )(*[pltpu.with_memory_space_constraint(x, pltpu.HBM) for x in operands])
    output, grad_query, grad_key, grad_value, grad_residue, grad_rate, grad_skip = pl.pallas_call(
        finish_kernel,
        out_shape=(wide,) * 4
        + (jax.ShapeDtypeStruct((1, modes), f32),) * 2
        + (jax.ShapeDtypeStruct((1, 1), f32),),
        in_specs=[vmem] * 11,
        out_specs=(vmem,) * 7,
        compiler_params=pltpu.CompilerParams(vmem_limit_bytes=32 * 2**20),
        name="finish",
    )(q, k, v, og, total, grad, row, *states)
    return (
        output, grad_query, grad_key, grad_value, grad_residue, grad_rate, grad_skip.reshape(1)
    )


def solution(mesh):
    wide = P(None, ("ctx", "sub"))
    rows = P(("ctx", "sub"), None)
    return jax.shard_map(
        body,
        mesh=mesh,
        in_specs=(wide, wide, wide, wide, rows, rows, P()),
        out_specs=(wide, wide, wide, wide, rows, rows, P(("ctx", "sub"))),
        check_vma=False,
    )
```

```python
import functools
import random

import jax
import jax.numpy as jnp
from jax import lax
from jax.experimental import pallas as pl
from jax.experimental.pallas import tpu as pltpu
from jax.sharding import PartitionSpec as P

MESH = pl.DeviceIdType.MESH
FULL = lax.Precision.HIGHEST
NT = (((1,), (1,)), ((), ()))
TN = (((0,), (0,)), ((), ()))
LANES = 128
GROUPS = 8


MOVES = [
    (x, y, z, core)
    for x in range(4) for y in range(4) for z in range(4) for core in range(2)
    if (x, y, z, core) != (0, 0, 0, 0)
]


def far_first(weights, ties):
    def key(move):
        hops = [min(step, 4 - step) for step in move[:3]]
        return (-sum(w * h for w, h in zip(weights, hops)), ties(move))

    found = {move: key(move) for move in MOVES}
    return sorted(MOVES, key=lambda move: found[move])


MIXED = far_first((1, 1, 1), lambda m: (m[0] * 37 + m[1] * 11 + m[2] * 23 + m[3] * 5) % 16)
FIRST_ROUND = far_first((0.5, 1, 1.5), lambda m, draw=random.Random(0): draw.random())
LAST_ROUND = far_first((1, 1, 1), lambda m, draw=random.Random(0): draw.random())


def iota(shape, axis):
    return lax.broadcasted_iota(jnp.int32, shape, axis)


def column(row):
    n = row.shape[1]
    eye = iota((n, n), 0) == iota((n, n), 1)
    return jnp.sum(jnp.where(eye, row, 0.0), axis=1, keepdims=True)


def as_row(col):
    n = col.shape[0]
    eye = iota((n, n), 0) == iota((n, n), 1)
    return jnp.sum(jnp.where(eye, col, 0.0), axis=0, keepdims=True)


def shifted(rows, count):
    n = rows.shape[0]
    if count > 0:
        moved = pltpu.roll(rows, count, 0)
        return jnp.where(iota(rows.shape, 0) >= count, moved, 0.0)
    moved = pltpu.roll(rows, n + count, 0)
    return jnp.where(iota(rows.shape, 0) < n + count, moved, 0.0)


def running(rows, speed, span, sign):
    n = rows.shape[0]
    step = 1
    while step < n:
        rows = rows + jnp.exp(-speed * float(span * step)) * shifted(rows, sign * step)
        step *= 2
    return shifted(rows, sign)


def partners(me, moves):
    core, z = me % 2, me // 4 % 4
    y, x = me // 2 % 2 * 2 + me // 16 % 2, me // 32
    across = [lax.rem(x + d, 4) * 8 for d in range(4)]
    along = [lax.rem(z + d, 4) for d in range(4)]
    ups = [lax.rem(y + d, 4) for d in range(4)]
    high = [[u // 2 * 2 + lax.rem(core + d, 2) for d in range(2)] for u in ups]
    low = [lax.rem(u, 2) * 4 for u in ups]
    found = []
    for dx, dy, dz, dc in moves:
        ctx, sub = across[dx] + low[dy] + along[dz], high[dy][dc]
        found.append((ctx * 4 + sub, (ctx, sub)))
    return found


def send_all(peers, me, src, dst, send_sem, recv_sem):
    for peer, place in peers:
        row = 0 if src.shape[0] == 1 else peer
        pltpu.make_async_remote_copy(
            src_ref=src.at[pl.ds(row, 1)],
            dst_ref=dst.at[pl.ds(me, 1)],
            send_sem=send_sem,
            recv_sem=recv_sem,
            device_id=place,
            device_id_type=MESH,
        ).start()


def whole(peers, dst, send_sem, recv_sem):
    return pltpu.make_async_remote_copy(
        src_ref=dst.at[pl.ds(0, len(peers))],
        dst_ref=dst.at[pl.ds(0, len(peers))],
        send_sem=send_sem,
        recv_sem=recv_sem,
        device_id=peers[0][1],
        device_id_type=MESH,
    )


def loop_steps(count, unroll, step, carry):
    def some(i, carry):
        for j in range(unroll):
            carry = step(i * unroll + j, carry)
        return carry

    return lax.fori_loop(0, count // unroll, some, carry)


def tile_rows(step):
    return pl.ds(pl.multiple_of(step * GROUPS, GROUPS), GROUPS)


def scan_groups(x_ref, y_ref, steps, decays, gains, backward):
    def step(i, states):
        rows = tile_rows(steps - 1 - i if backward else i)
        x = x_ref[rows, :]
        states = [a * h + x for a, h in zip(decays, states)]
        y_ref[rows, :] = sum(g * h for g, h in zip(gains, states))
        return states

    start = [jnp.zeros((GROUPS, LANES), jnp.float32)] * len(decays)
    return loop_steps(steps, 4, step, start)


def add_states(y_ref, steps, decays, states, backward):
    def step(i, states):
        rows = tile_rows(steps - 1 - i if backward else i)
        states = [a * s for a, s in zip(decays, states)]
        y_ref[rows, :] = y_ref[rows, :] + sum(states)
        return states

    loop_steps(steps, 8, step, states)


def natural(y_ref, steps, j):
    per_block = LANES // steps
    parts = [
        y_ref[pl.ds(j * per_block + g, steps, stride=GROUPS), :] for g in range(per_block)
    ]
    return jnp.concatenate(parts, axis=0).T


def exchange_kernel(
    devices, sub, q_hbm, k_hbm, v_hbm, og_hbm, res_hbm, rate_hbm, gain_hbm,
    sum_ref, grad_ref, row_ref, q_ref, k_ref, v_ref, og_ref, state_ref, factor_ref, rise_ref,
    fall_ref, gain_ref, res_ref, rate_ref, stage, out_buf, in_buf, par_buf, par_all, state_buf,
    mixed_t, gated_t, conv_t, corr_t,
    load_sems, out_send, out_recv, par_send, par_recv, state_send, state_recv,
):
    me = lax.axis_index("ctx") * sub + lax.axis_index("sub")
    channels, width = q_ref.shape
    blocks = width // LANES
    steps = width // GROUPS
    slab = 2 * blocks
    modes = res_ref.shape[1]
    f32, bf16 = jnp.float32, jnp.bfloat16
    peers = partners(me, MIXED)
    barrier = pltpu.get_barrier_semaphore()
    for _, place in peers:
        pl.semaphore_signal(barrier, inc=1, device_id=place, device_id_type=MESH)
    loads = [
        pltpu.make_async_copy(src, dst, load_sems.at[i])
        for i, (src, dst) in enumerate(
            [(k_hbm, k_ref), (v_hbm, v_ref), (og_hbm, og_ref), (q_hbm, q_ref),
             (res_hbm, res_ref), (rate_hbm, rate_ref), (gain_hbm, gain_ref)]
        )
    ]
    for load in loads:
        load.start()
    for load in loads:
        load.wait()

    mixed_own = k_ref[...].astype(f32) * v_ref[...].astype(f32)
    gated_own = og_ref[...].astype(f32) * q_ref[...].astype(f32)
    for j in range(blocks):
        cols = slice(j * LANES, (j + 1) * LANES)
        stage[pl.ds(j, channels, stride=slab), :] = mixed_own[:, cols]
        stage[pl.ds(blocks + j, channels, stride=slab), :] = gated_own[:, cols]
    out_buf[...] = stage[...].astype(bf16).reshape(channels, slab, LANES)
    speed_row = jnp.exp(rate_ref[...])
    res_row = res_ref[...]
    par_buf[...] = jnp.zeros((1, LANES), f32)
    par_buf[:, 0:modes] = speed_row
    par_buf[:, modes : 2 * modes] = res_row

    pl.semaphore_wait(barrier, devices - 1)
    send_all(partners(me, FIRST_ROUND), me, out_buf, in_buf, out_send, out_recv)
    send_all(peers, me, par_buf, par_all, par_send, par_recv)
    in_buf[me] = out_buf[me]
    par_all[pl.ds(me, 1), :] = par_buf[...]

    speed = column(speed_row)
    copies = LANES // modes
    half = copies // 2
    wide_speed = as_row(jnp.concatenate([speed] * copies, axis=0))
    pos = iota((modes, width), 1).astype(f32)
    rise = jnp.exp(-speed * pos)
    fall = jnp.exp(-speed * (width - 1.0 - pos))
    blank = jnp.zeros((half * modes, width), f32)
    to_end = jnp.concatenate([fall] * half + [blank], axis=0).astype(bf16)
    to_start = jnp.concatenate([blank] + [rise] * half, axis=0).astype(bf16)
    to_end_timed = (fall * (width - 1.0 - pos)).astype(bf16)
    to_start_timed = (rise * pos).astype(bf16)
    grow = jnp.exp(speed * iota((modes, LANES), 1).astype(f32))
    mixed_own = (k_ref[...].astype(f32) * v_ref[...].astype(f32)).astype(bf16).astype(f32)
    gated_own = (og_ref[...].astype(f32) * q_ref[...].astype(f32)).astype(bf16).astype(f32)
    per_block = LANES // steps
    for own, turned in ((mixed_own, mixed_t), (gated_own, gated_t)):
        for j in range(blocks):
            block = own[:, j * LANES : (j + 1) * LANES].T
            for g in range(per_block):
                turned[pl.ds(j * per_block + g, steps, stride=GROUPS), :] = block[
                    g * steps : (g + 1) * steps, :
                ]

    whole(peers, in_buf, out_send, out_recv).wait_recv()
    stage[...] = in_buf[...].reshape(devices * slab, LANES).astype(f32)

    def gathered(start):
        parts = [stage[pl.ds(start + j, devices, stride=slab), :] for j in range(blocks)]
        return jnp.concatenate(parts, axis=1).astype(bf16)

    mixed, gated = gathered(0), gathered(blocks)

    def state(rows, weights):
        return lax.dot_general(rows, weights, NT, preferred_element_type=f32)

    ends, starts = state(mixed, to_end), state(gated, to_start)
    before = running(ends, wide_speed, width, 1)
    after = running(starts, wide_speed, width, -1)
    state_buf[...] = before + after
    send_all(partners(me, LAST_ROUND), me, state_buf, state_ref, state_send, state_recv)
    state_ref[pl.ds(me, 1), :] = state_buf[pl.ds(me, 1), :]

    whole(peers, par_all, par_send, par_recv).wait_recv()
    params = par_all[...].T
    speeds = [jnp.broadcast_to(params[r : r + 1, :], (GROUPS, LANES)) for r in range(modes)]
    gains = [
        jnp.broadcast_to(params[modes + r : modes + r + 1, :], (GROUPS, LANES))
        for r in range(modes)
    ]
    decays = [jnp.exp(-x) for x in speeds]
    gain = column(gain_ref[...])
    for backward, own, x_ref, y_ref, to_ref in (
        (False, mixed_own, mixed_t, conv_t, sum_ref), (True, gated_own, gated_t, corr_t, grad_ref)
    ):
        found = scan_groups(x_ref, y_ref, steps, decays, gains, backward)
        sign = -1 if backward else 1
        inner = []
        for r in range(modes):
            sums = found[r]
            step = 1
            while step < GROUPS:
                sums = sums + jnp.exp(-speeds[r] * float(steps * step)) * shifted(sums, sign * step)
                step *= 2
            inner.append(gains[r] * shifted(sums, sign))
        add_states(y_ref, steps, decays, inner, backward)
        for j in range(blocks):
            cols = slice(j * LANES, (j + 1) * LANES)
            to_ref[:, cols] = natural(y_ref, steps, j) + gain * own[:, cols]

    lane = iota((channels, LANES), 1)
    own_gain = jnp.where((lane >= modes) & (lane < 2 * modes), par_all[...], 0.0)
    own_gain = pltpu.roll(own_gain, LANES - modes, 1)
    own_speed = jnp.where(lane < modes, par_all[...], 0.0)
    step = modes
    while step < LANES:
        own_gain = own_gain + pltpu.roll(own_gain, step, 1)
        own_speed = own_speed + pltpu.roll(own_speed, step, 1)
        step *= 2
    home = iota((channels, LANES), 0) % (2 * copies) - lane // modes
    for n in range(blocks):
        scaled = own_gain * jnp.exp(-own_speed * float(n * LANES))
        factor_ref[n, :, :LANES] = jnp.where(home == 0, scaled, 0.0).astype(bf16)
        factor_ref[n, :, LANES:] = jnp.where(home == copies, scaled, 0.0).astype(bf16)
    ahead = (iota((modes, LANES), 1) + 1).astype(f32)
    behind = (LANES - iota((modes, LANES), 1)).astype(f32)
    for c in range(channels):
        rate = -params[:modes, c : c + 1]
        rows = slice(c * modes, (c + 1) * modes)
        rise_ref[rows, :] = jnp.exp(rate * ahead).astype(bf16)
        fall_ref[rows, :] = jnp.exp(rate * behind).astype(bf16)

    pairs = lax.dot_general(mixed, gated, TN, preferred_element_type=f32)
    lag = iota((LANES, width), 1) - iota((LANES, width), 0)
    lagged = []
    for k in range(blocks):
        total = pairs[:LANES, k * LANES : (k + 1) * LANES]
        for row in range(1, blocks - k):
            rows = slice(row * LANES, (row + 1) * LANES)
            total = total + pairs[rows, (row + k) * LANES : (row + k + 1) * LANES]
        lagged.append(total)
    lagged = jnp.where(lag >= 0, jnp.concatenate(lagged, axis=1), 0.0)
    skip_sum = jnp.sum(jnp.where(lag == 0, lagged, 0.0), keepdims=True)

    def local_sum(values):
        by_lag = jnp.dot(grow, values, precision=FULL, preferred_element_type=f32)
        return jnp.sum(by_lag * rise, axis=1, keepdims=True)

    plain_col = local_sum(lagged)
    timed_col = local_sum(lagged * lag.astype(f32))
    one_step = jnp.exp(-speed_row)
    chunk_step = jnp.exp(-speed_row * float(width))
    ends_timed, starts_timed = state(mixed, to_end_timed), state(gated, to_start_timed)
    first, second = slice(0, modes), slice(half * modes, (half + 1) * modes)
    before, after, starts = before[:, first], after[:, second], starts[:, second]
    cross = before * starts
    cross_timed = ends_timed * after + before * starts_timed + cross
    cross_timed = cross_timed + (float(width) * chunk_step) * (before * after)
    plain = as_row(plain_col) + one_step * jnp.sum(cross, axis=0, keepdims=True)
    timed = as_row(timed_col) + one_step * jnp.sum(cross_timed, axis=0, keepdims=True)
    seq_len = devices * width
    row_ref[0:1, :] = jnp.zeros((1, LANES), f32)
    row_ref[0:1, 0:modes] = plain * (1.0 / seq_len)
    row_ref[0:1, modes : 2 * modes] = -res_row * speed_row * timed * (1.0 / seq_len**0.5)
    row_ref[0:1, 2 * modes : 2 * modes + 1] = skip_sum

    whole(peers, in_buf, out_send, out_recv).wait_send()
    whole(peers, par_all, par_send, par_recv).wait_send()
    whole(peers, state_ref, state_send, state_recv).wait_recv()
    whole(peers, state_ref, state_send, state_recv).wait_send()


def finish_kernel(
    q_ref, k_ref, v_ref, og_ref, sum_ref, grad_ref, row_ref, state_ref, factor_ref, rise_ref,
    fall_ref, out_ref, gq_ref, gk_ref, gv_ref, gres_ref, grate_ref, gskip_ref,
):
    f32, bf16 = jnp.float32, jnp.bfloat16
    channels, width = q_ref.shape
    modes = gres_ref.shape[1]
    copies = LANES // modes
    gres_ref[...] = row_ref[:, 0:modes]
    grate_ref[...] = row_ref[:, modes : 2 * modes]
    gskip_ref[...] = row_ref[:, 2 * modes : 2 * modes + 1]
    blocks = width // LANES
    tall = 2 * copies
    states = state_ref[...]
    other = pltpu.roll(states, LANES // 2, 1)
    first = iota((channels, LANES), 1) < LANES // 2
    before = jnp.where(first, states, other).astype(bf16)
    after = jnp.where(first, other, states).astype(bf16)
    for g in range(channels // tall):
        rows = slice(g * tall, (g + 1) * tall)
        deep = slice(g * tall * modes, (g + 1) * tall * modes)
        for found, order, table_ref, base_ref, pair, places in (
            (before, 1, rise_ref, sum_ref, (q_ref, og_ref), (out_ref, gq_ref)),
            (after, -1, fall_ref, grad_ref, (v_ref, k_ref), (gk_ref, gv_ref)),
        ):
            own = jnp.concatenate([found[rows, :]] * 2, axis=1)
            parts = [own * factor_ref[n, rows, :] for n in range(blocks)][::order]
            share = jnp.dot(
                jnp.concatenate(parts, axis=0),
                table_ref[deep, :],
                preferred_element_type=f32,
            )
            for n in range(blocks):
                cols = slice(n * LANES, (n + 1) * LANES)
                total = share[n * tall : (n + 1) * tall, :] + base_ref[rows, cols]
                for factor, place in zip(pair, places):
                    place[rows, cols] = (factor[rows, cols].astype(f32) * total).astype(bf16)


def body(queries, key_branch, value_branch, out_grad, residue, log_rate, skip_gain):
    sub = lax.axis_size("sub")
    devices = lax.axis_size("ctx") * sub
    channels, width = queries.shape
    modes = residue.shape[1]
    slab = 2 * width // LANES
    f32, bf16 = jnp.float32, jnp.bfloat16
    vmem = pl.BlockSpec(memory_space=pltpu.VMEM)
    wide = jax.ShapeDtypeStruct((channels, width), bf16)
    full = jax.ShapeDtypeStruct((channels, width), f32)
    square = jax.ShapeDtypeStruct((channels, LANES), f32)
    table = jax.ShapeDtypeStruct((channels * modes, LANES), bf16)
    factors = jax.ShapeDtypeStruct((width // LANES, channels, 2 * LANES), bf16)
    hbm = pl.BlockSpec(memory_space=pltpu.HBM)
    operands = (queries, key_branch, value_branch, out_grad, residue, log_rate, skip_gain[None, :])
    total, grad, row, q, k, v, og, *states = pl.pallas_call(
        functools.partial(exchange_kernel, devices, sub),
        out_shape=(
            full, full, jax.ShapeDtypeStruct((1, LANES), f32), wide, wide, wide, wide,
            square, factors, table, table,
        ),
        in_specs=[hbm] * 7,
        out_specs=(vmem,) * 11,
        scratch_shapes=[
            pltpu.VMEM((1, channels), f32),
            pltpu.VMEM((1, modes), f32),
            pltpu.VMEM((1, modes), f32),
            pltpu.VMEM((channels * slab, LANES), f32),
            pltpu.VMEM((channels, slab, LANES), bf16),
            pltpu.VMEM((devices, slab, LANES), bf16),
            pltpu.VMEM((1, LANES), f32),
            pltpu.VMEM((channels, LANES), f32),
            pltpu.VMEM((devices, LANES), f32),
            pltpu.VMEM((width, LANES), f32),
            pltpu.VMEM((width, LANES), f32),
            pltpu.VMEM((width, LANES), f32),
            pltpu.VMEM((width, LANES), f32),
            pltpu.SemaphoreType.DMA((7,)),
            pltpu.SemaphoreType.DMA,
            pltpu.SemaphoreType.DMA,
            pltpu.SemaphoreType.DMA,
            pltpu.SemaphoreType.DMA,
            pltpu.SemaphoreType.DMA,
            pltpu.SemaphoreType.DMA,
        ],
        compiler_params=pltpu.CompilerParams(
            collective_id=0, has_side_effects=True, vmem_limit_bytes=32 * 2**20
        ),
        name="exchange",
    )(*[pltpu.with_memory_space_constraint(x, pltpu.HBM) for x in operands])
    output, grad_query, grad_key, grad_value, grad_residue, grad_rate, grad_skip = pl.pallas_call(
        finish_kernel,
        out_shape=(wide,) * 4
        + (jax.ShapeDtypeStruct((1, modes), f32),) * 2
        + (jax.ShapeDtypeStruct((1, 1), f32),),
        in_specs=[vmem] * 11,
        out_specs=(vmem,) * 7,
        compiler_params=pltpu.CompilerParams(vmem_limit_bytes=32 * 2**20),
        name="finish",
    )(q, k, v, og, total, grad, row, *states)
    return (
        output, grad_query, grad_key, grad_value, grad_residue, grad_rate, grad_skip.reshape(1)
    )


def solution(mesh):
    wide = P(None, ("ctx", "sub"))
    rows = P(("ctx", "sub"), None)
    return jax.shard_map(
        body,
        mesh=mesh,
        in_specs=(wide, wide, wide, wide, rows, rows, P()),
        out_specs=(wide, wide, wide, wide, rows, rows, P(("ctx", "sub"))),
        check_vma=False,
    )
```
